512 devices in a mesh: fsdp: 64 (over x, y, core), tp: 8 (over z).
Axes of the slice: x: 4, y: 8, z: 8, core: 2. Of those that a mesh axis runs over, the one named last changes fastest.
Arguments:
- mom_up: float32 [3072, 12288], P('fsdp', 'tp'), may hold values from -6 to 6
- grad_up: bfloat16 [3072, 12288], P('fsdp', 'tp'), may hold values from -150 to 150
- basis_up: float32 [8, 1536, 256], P('tp', 'fsdp'), may hold values from -6 to 6
- mom_down: float32 [12288, 3072], P('fsdp', 'tp'), may hold values from -6 to 6
- grad_down: bfloat16 [12288, 3072], P('fsdp', 'tp'), may hold values from -150 to 150
- basis_down: float32 [8, 384, 256], P('tp', 'fsdp'), may hold values from -6 to 6
Outputs:
- update_up: float32 [3072, 12288], P('fsdp', 'tp')
- next_mom_up: float32 [3072, 12288], P('fsdp', 'tp')
- next_basis_up: float32 [8, 1536, 256], P('tp', 'fsdp')
- update_down: float32 [12288, 3072], P('fsdp', 'tp')
- next_mom_down: float32 [12288, 3072], P('fsdp', 'tp')
- next_basis_down: float32 [8, 384, 256], P('tp', 'fsdp')
The draws below stay inside these ranges and needn't reach their ends.
All inputs are finite; a program needn't handle non-finite values.
Results may differ from the reference program's by a relative error of at most 0.00055.
Values sent between devices are 32-bit elements; how exact they have to be, the bound alone decides.
A program may use at most 64 MiB of HBM per device.

```python
import math
import jax
import jax.numpy as jnp
from jax import lax

D = 3072
FF = 12288
RANK = 256
N_TP = 8


def scaled_field(key, rows, cols, row_top):
    first, second, third = jax.random.split(key, 3)
    base = jnp.clip(jax.random.normal(first, (rows, cols), jnp.float32), -5.0, 5.0)
    row_scale = jnp.exp(jax.random.uniform(second, (rows, 1), jnp.float32, 0.0, math.log(row_top)))
    trend = jnp.exp(math.log(3.0) * jnp.arange(rows, dtype=jnp.float32)[:, None] / rows)
    col_scale = jnp.exp(jax.random.uniform(third, (1, cols), jnp.float32, 0.0, math.log(10.0)))
    return base * row_scale * trend * col_scale / 10.0


def draw_grad_up(key, part):
    key = jax.random.fold_in(key, 11)
    values = scaled_field(key, D, FF, 10.0)
    return values.astype(jnp.bfloat16)


def draw_grad_down(key, part):
    key = jax.random.fold_in(key, 23)
    values = scaled_field(key, FF, D, 10.0)
    return values.astype(jnp.bfloat16)


def block_scale(rng, dims, shards, low, largest):
    level, own = 1.0, jax.random.fold_in(rng, 6)
    for dim, shards_of in shards:
        draws = jnp.exp(jax.random.uniform(jax.random.fold_in(own, dim), (shards_of,), jnp.float32, low / len(shards), largest / len(shards)))
        level = level * jnp.repeat(draws, dims[dim] // shards_of).reshape([-1 if axis == dim else 1 for axis in range(len(dims))])
    return level


def bell_draw(own_key, extent, spread, most, cuts=(), kind=jnp.bfloat16):
    result = jax.random.normal(own_key, extent, jnp.float32) * spread
    if len(cuts) > 0:
        result = block_scale(own_key, extent, cuts, -0.22, 0.18) * result
    return jnp.clip(result, min=-most, max=most).astype(kind)


def setup_inputs(seed: int = 0) -> dict:
    seeds = jax.random.split(jax.random.key(seed), 7)
    mom_up = bell_draw(seeds[0], (D, FF), 1.0, 6.0, ((0, 64), (1, 8)), jnp.float32)
    grad_up = draw_grad_up(jax.random.fold_in(seeds[6], 71), 0)
    basis_up = bell_draw(seeds[2], (N_TP, FF // N_TP, RANK), 1.0, 6.0, ((0, 8), (1, 64)), jnp.float32)
    mom_down = bell_draw(seeds[3], (FF, D), 1.0, 6.0, ((0, 64), (1, 8)), jnp.float32)
    grad_down = draw_grad_down(jax.random.fold_in(seeds[6], 71), 0)
    basis_down = bell_draw(seeds[5], (N_TP, D // N_TP, RANK), 1.0, 6.0, ((0, 8), (1, 64)), jnp.float32)
    return dict(mom_up=mom_up, grad_up=grad_up, basis_up=basis_up, mom_down=mom_down, grad_down=grad_down, basis_down=basis_down)


retain = 0.9
epsilon = 1e-06
HIGH = lax.Precision.HIGHEST

def dion_matrix(mom, grad, basis):
    rows, cols = mom.shape
    width = basis.shape[2]
    right_basis = basis.reshape(cols, width)
    blended = mom + grad.astype(jnp.float32)
    projected = jnp.dot(blended.astype(jnp.float32), right_basis.astype(jnp.float32), precision=HIGH, preferred_element_type=jnp.float32)
    gram = jnp.dot(projected.T.astype(jnp.float32), projected.astype(jnp.float32), precision=HIGH, preferred_element_type=jnp.float32)
    lower = jnp.linalg.cholesky(gram)
    ortho = lax.linalg.triangular_solve(lower, projected, left_side=False, lower=True, transpose_a=True)
    right = jnp.dot(blended.T.astype(jnp.float32), ortho.astype(jnp.float32), precision=HIGH, preferred_element_type=jnp.float32)
    next_mom = blended - (1.0 - retain) * jnp.dot(ortho.astype(jnp.float32), right.T.astype(jnp.float32), precision=HIGH, preferred_element_type=jnp.float32)
    scale = lax.rsqrt(lax.optimization_barrier(jnp.sum(right * right, axis=0)) + epsilon)
    next_basis = right * scale[None, :]
    update = math.sqrt(rows / cols) * jnp.dot(ortho.astype(jnp.float32), next_basis.T.astype(jnp.float32), precision=HIGH, preferred_element_type=jnp.float32)
    return (update, next_mom, next_basis.reshape(basis.shape))

def reference(mom_up, grad_up, basis_up, mom_down, grad_down, basis_down):
    update_up, next_mom_up, next_basis_up = dion_matrix(mom_up, grad_up, basis_up)
    update_down, next_mom_down, next_basis_down = dion_matrix(mom_down, grad_down, basis_down)
    return (update_up, next_mom_up, next_basis_up, update_down, next_mom_down, next_basis_down)
```

```python
import math

import jax
import jax.numpy as jnp
from jax import lax
from jax.experimental import pallas as pl
from jax.experimental.pallas import tpu as pltpu
from jax.sharding import PartitionSpec as P

retain = 0.9
epsilon = 1e-06
HIGH = lax.Precision.HIGHEST
MESH = pl.DeviceIdType.MESH
NX, NY, NZ, RANK = 4, 8, 8, 256
F32 = jnp.float32


def dot(a, b, ca=1, cb=0):
    return lax.dot_general(
        a, b, (((ca,), (cb,)), ((), ())), precision=HIGH, preferred_element_type=F32
    )


def invert_half(a):
    lanes = lax.broadcasted_iota(jnp.int32, (8, 128), 1)
    subs = lax.broadcasted_iota(jnp.int32, (8, 128), 0)
    groups = [a[8 * g : 8 * g + 8] for g in range(16)]
    done = []
    for k in range(16):
        base = 8 * k
        inside = (lanes >= base) & (lanes < base + 8)
        panel = groups[0]
        cols = [jnp.broadcast_to(panel[:, base + j : base + j + 1], (8, 128)) for j in range(8)]
        held = jnp.where(inside, (lanes == subs + base).astype(F32), panel)
        pivots = cols[0]
        inverse, heads = [], []
        for j in range(8):
            r = 1.0 / cols[j][j : j + 1]
            inverse.append(r)
            mult = jnp.where(subs > j, cols[j] * r, 0.0)
            heads.append([c[j : j + 1] for c in cols])
            for jj in range(j + 1, 8):
                cols[jj] = cols[jj] - mult * heads[j][jj]
            held = held - mult * held[j : j + 1]
            if j:
                pivots = jnp.where(subs == j, cols[j], pivots)
        done.append(jnp.where(lanes <= subs + base, held * lax.rsqrt(pivots), 0.0))
        rest = []
        for g in groups[1:]:
            c = [jnp.broadcast_to(g[:, base + j : base + j + 1], (8, 128)) for j in range(8)]
            out = jnp.where(inside, 0.0, g)
            for j in range(8):
                m = c[j] * inverse[j]
                for jj in range(j + 1, 8):
                    c[jj] = c[jj] - m * heads[j][jj]
                out = out - m * held[j : j + 1]
            rest.append(out)
        groups = rest
    return jnp.concatenate(done, axis=0)


def place():
    f = lax.axis_index("fsdp")
    return f // 16, lax.rem(f // 2, 8), lax.rem(f, 2), lax.axis_index("tp")


def kernel(
    mom_up, grad_up, basis_up, mom_down, grad_down, basis_down,
    upd_up, new_up, nb_up, upd_down, new_down, nb_down,
    q, blend_up, blend_down, padded,
    part, part_in, pfull,
    gram, gram_in, gsum, g_x, g_xs, g_y, g_all,
    wpart, wcore, wsum, wu_x, wu_s, wu_y, wd_y, wd_s, wd_x, wfull,
    xinv, ssum, ssum_in,
    send, recv,
):
    x, y, c, z = place()
    count = [0]

    def at(xx, yy, cc, zz):
        return (xx * 16 + yy * 2 + cc, zz)

    def along_y(d):
        return at(x, lax.rem(y + d, NY), c, z)

    def along_x(d):
        return at(lax.rem(x + d, NX), y, c, z)

    def along_z(d):
        return at(x, y, c, lax.rem(z + d, NZ))

    sibling = at(x, y, 1 - c, z)

    barrier = pltpu.get_barrier_semaphore()
    peers = (
        [along_y(d) for d in range(1, NY)]
        + [along_x(d) for d in range(1, NX)]
        + [along_z(d) for d in range(1, NZ)]
        + [sibling]
    )
    for peer in peers:
        pl.semaphore_signal(barrier, inc=1, device_id=peer, device_id_type=MESH)

    started = []

    def transfer(src, dst, device, arrives):
        n = count[0]
        count[0] += 1
        copy = pltpu.make_async_remote_copy(
            src, dst, send.at[n], recv.at[n], device_id=device, device_id_type=MESH
        )
        copy.start()
        started.append(copy)
        landing = pltpu.make_async_remote_copy(
            src, arrives, send.at[n], recv.at[n], device_id=device, device_id_type=MESH
        )
        return landing.wait_recv

    def wait(waits):
        for w in waits:
            w()

    def back(v, d, n):
        return lax.rem(v + n - d, n)

    q[x, y, c, 0:24, :] = basis_up[0]
    q[x, y, c, 24:32, :] = jnp.zeros((8, RANK), F32)
    q[x, y, c, 24:30, :] = basis_down[0]
    pl.semaphore_wait(barrier, len(peers))

    def gather_start(buf):
        up_y = [
            transfer(buf.at[x, y, c, 0:24], buf.at[x, y, c, 0:24], along_y(d),
                     buf.at[x, back(y, d, NY), c, 0:24])
            for d in range(1, NY)
        ]
        down_x = [
            transfer(buf.at[x, y, c, 24:32], buf.at[x, y, c, 24:32], along_x(d),
                     buf.at[back(x, d, NX), y, c, 24:32])
            for d in range(1, NX)
        ]
        return up_y, down_x

    def gather_end(buf, up_y, down_x):
        wait(down_x)
        down_y = [
            transfer(buf.at[:, y, c, 24:32], buf.at[:, y, c, 24:32], along_y(d),
                     buf.at[:, back(y, d, NY), c, 24:32])
            for d in range(1, NY)
        ]
        wait(up_y)
        up_x = [
            transfer(buf.at[x, :, c, 0:24], buf.at[x, :, c, 0:24], along_x(d),
                     buf.at[back(x, d, NX), :, c, 0:24])
            for d in range(1, NX)
        ]
        wait(down_y)
        wait(up_x)
        wait([transfer(buf.at[:, :, c], buf.at[:, :, c], sibling, buf.at[:, :, 1 - c])])

    first = gather_start(q)
    blend_up[...] = mom_up[...] + grad_up[...].astype(F32)
    blend_down[...] = mom_down[...] + grad_down[...].astype(F32)
    column = lax.broadcasted_iota(jnp.int32, (384, 512), 0)
    slot = lax.broadcasted_iota(jnp.int32, (384, 512), 1)
    pick = ((column == (slot // 8) * 6 + lax.rem(slot, 8)) & (lax.rem(slot, 8) < 6)).astype(F32)
    padded[...] = dot(blend_down[...], pick)
    gather_end(q, *first)

    p_up = dot(blend_up[...], q[:, :, :, 0:24, :].reshape(1536, RANK))
    p_down = dot(padded[...], q[:, :, :, 24:32, :].reshape(512, RANK))
    part[:, 0:24, :] = p_down.reshape(8, 24, RANK)
    part[0:6, 24:32, :] = p_up.reshape(6, 8, RANK)
    part[6:8, 24:32, :] = jnp.zeros((2, 8, RANK), F32)
    wait([
        transfer(part.at[lax.rem(z + d, NZ)], part_in.at[d - 1], along_z(d), part_in.at[d - 1])
        for d in range(1, NZ)
    ])
    total = part[z]
    for d in range(1, NZ):
        total = total + part_in[d - 1]
    pfull[z] = total
    wait([
        transfer(pfull.at[z], pfull.at[z], along_z(d), pfull.at[back(z, d, NZ)])
        for d in range(1, NZ)
    ])
    p_up = pfull[0:6, 24:32, :].reshape(48, RANK)
    p_down = pfull[:, 0:24, :].reshape(192, RANK)

    gram[0] = dot(p_up, p_up, 0, 0)
    gram[1] = dot(p_down, p_down, 0, 0)
    gram_wait = transfer(gram.at[1 - c], gram_in, sibling, gram_in)
    wpart[:, :, :, 0:24, :] = dot(blend_up[...], p_up, 0, 0).reshape(NX, NY, 2, 24, RANK)
    wpart[:, :, :, 24:32, :] = dot(padded[...], p_down, 0, 0).reshape(NX, NY, 2, 8, RANK)
    gram_wait()
    gsum[...] = (gram[c] + gram_in[...]).reshape(NX, 64, RANK)
    wait([
        transfer(gsum.at[lax.rem(x + d, NX)], g_x.at[d - 1], along_x(d), g_x.at[d - 1])
        for d in range(1, NX)
    ])
    g_xs[...] = (gsum[x] + g_x[0] + g_x[1] + g_x[2]).reshape(NY, 8, RANK)
    wait([
        transfer(g_xs.at[lax.rem(y + d, NY)], g_y.at[d - 1], along_y(d), g_y.at[d - 1])
        for d in range(1, NY)
    ])
    row = g_xs[y]
    for d in range(1, NY):
        row = row + g_y[d - 1]
    g_all[x, y] = row
    wait([
        transfer(g_all.at[x, y], g_all.at[x, y], along_y(d), g_all.at[x, back(y, d, NY)])
        for d in range(1, NY)
    ])
    g_wait = [
        transfer(g_all.at[x], g_all.at[x], along_x(d), g_all.at[back(x, d, NX)])
        for d in range(1, NX)
    ]

    core_wait = transfer(wpart.at[:, :, 1 - c], wcore, sibling, wcore)
    core_wait()
    wsum[...] = wpart[:, :, c] + wcore[...]
    wait(g_wait)
    up_x = [
        transfer(wsum.at[lax.rem(x + d, NX), :, 0:24], wu_x.at[d - 1], along_x(d), wu_x.at[d - 1])
        for d in range(1, NX)
    ]
    down_y = [
        transfer(wsum.at[:, lax.rem(y + d, NY), 24:32], wd_y.at[d - 1], along_y(d), wd_y.at[d - 1])
        for d in range(1, NY)
    ]

    g11, g12, g22 = (
        g_all[0:2, :, :, 0:128].reshape(128, 128),
        g_all[0:2, :, :, 128:256].reshape(128, 128),
        g_all[2:4, :, :, 128:256].reshape(128, 128),
    )
    x11 = invert_half(g11)
    xinv[c, 0:128, 0:128] = x11
    xinv[c, 0:128, 128:256] = jnp.zeros((128, 128), F32)
    u = dot(x11, g12)
    low = g22 - dot(u, u, 0, 0)
    corner = dot(u, x11, 0, 0)

    wait(up_x)
    wu_s[...] = wsum[x, :, 0:24] + wu_x[0] + wu_x[1] + wu_x[2]
    up_y = [
        transfer(wu_s.at[lax.rem(y + d, NY)], wu_y.at[d - 1], along_y(d), wu_y.at[d - 1])
        for d in range(1, NY)
    ]
    wait(down_y)
    owned = wsum[:, y, 24:32]
    for d in range(1, NY):
        owned = owned + wd_y[d - 1]
    wd_s[...] = owned
    down_x = [
        transfer(wd_s.at[lax.rem(x + d, NX)], wd_x.at[d - 1], along_x(d), wd_x.at[d - 1])
        for d in range(1, NX)
    ]

    x22 = invert_half(low)
    xinv[c, 128:256, 128:256] = x22
    xinv[c, 128:256, 0:128] = -dot(x22, corner)
    x_wait = transfer(xinv.at[c], xinv.at[c], sibling, xinv.at[1 - c])

    wait(up_y)
    owned = wu_s[y]
    for d in range(1, NY):
        owned = owned + wu_y[d - 1]
    wfull[x, y, c, 0:24, :] = owned
    wait(down_x)
    wfull[x, y, c, 24:32, :] = wd_s[x] + wd_x[0] + wd_x[1] + wd_x[2]
    second = gather_start(wfull)
    x_wait()
    o_up = dot(p_up, xinv[0], 1, 1)
    o_down = dot(p_down, xinv[1], 1, 1)
    gather_end(wfull, *second)

    right_up = dot(wfull[:, :, :, 0:24, :].reshape(1536, RANK), xinv[0], 1, 1)
    right_down = dot(dot(pick, wfull[:, :, :, 24:32, :].reshape(512, RANK)), xinv[1], 1, 1)
    ssum[...] = jnp.zeros((8, RANK), F32)
    ssum[0:1, :] = jnp.sum(right_up * right_up, axis=0, keepdims=True)
    ssum[1:2, :] = jnp.sum(right_down * right_down, axis=0, keepdims=True)
    s_wait = [
        transfer(ssum, ssum_in.at[d - 1], along_z(d), ssum_in.at[d - 1]) for d in range(1, NZ)
    ]
    new_up[...] = blend_up[...] - (1.0 - retain) * dot(o_up, right_up, 1, 1)
    new_down[...] = blend_down[...] - (1.0 - retain) * dot(o_down, right_down, 1, 1)
    wait(s_wait)
    sums = ssum[...]
    for d in range(1, NZ):
        sums = sums + ssum_in[d - 1]
    scale = lax.rsqrt(sums + epsilon)
    s_up, s_down = scale[0:1], scale[1:2]
    upd_up[...] = math.sqrt(3072 / 12288) * dot(o_up * s_up, right_up, 1, 1)
    upd_down[...] = math.sqrt(12288 / 3072) * dot(o_down * s_down, right_down, 1, 1)
    nb_up[0] = dot(wfull[x, y, c, 0:24, :], xinv[0], 1, 1) * s_up
    nb_down[0] = (dot(wfull[x, y, c, 24:32, :], xinv[1], 1, 1) * s_down)[0:6]
    for copy in started:
        copy.wait_send()


SCRATCH = (
    [(NX, NY, 2, 32, RANK), (48, 1536), (192, 384), (192, 512)]
    + [(NZ, 32, RANK), (NZ - 1, 32, RANK), (NZ, 32, RANK)]
    + [(2, RANK, RANK), (RANK, RANK), (NX, 64, RANK), (NX - 1, 64, RANK), (NY, 8, RANK)]
    + [(NY - 1, 8, RANK), (NX, NY, 8, RANK)]
    + [(NX, NY, 2, 32, RANK), (NX, NY, 32, RANK), (NX, NY, 32, RANK)]
    + [(NX - 1, NY, 24, RANK), (NY, 24, RANK), (NY - 1, 24, RANK)]
    + [(NY - 1, NX, 8, RANK), (NX, 8, RANK), (NX - 1, 8, RANK), (NX, NY, 2, 32, RANK)]
    + [(2, RANK, RANK), (8, RANK), (NZ - 1, 8, RANK)]
)
COPIES = 128


def body(*args):
    vmem = pl.BlockSpec(memory_space=pltpu.VMEM)
    shapes = [(48, 1536), (48, 1536), (1, 24, RANK), (192, 384), (192, 384), (1, 6, RANK)]
    return pl.pallas_call(
        kernel,
        out_shape=[jax.ShapeDtypeStruct(s, F32) for s in shapes],
        in_specs=[vmem] * 6,
        out_specs=[vmem] * 6,
        scratch_shapes=[pltpu.VMEM(s, F32) for s in SCRATCH]
        + [pltpu.SemaphoreType.DMA((COPIES,))] * 2,
        compiler_params=pltpu.CompilerParams(
            collective_id=0, has_side_effects=True, vmem_limit_bytes=56 << 20
        ),
    )(*args)


def solution(mesh):
    specs = (P("fsdp", "tp"), P("fsdp", "tp"), P("tp", "fsdp", None)) * 2
    return jax.shard_map(
        body,
        mesh=mesh,
        in_specs=specs,
        out_specs=specs,
        check_vma=False,
    )
```

```python
import math

import jax
import jax.numpy as jnp
from jax import lax
from jax.experimental import pallas as pl
from jax.experimental.pallas import tpu as pltpu
from jax.sharding import PartitionSpec as P

retain = 0.9
epsilon = 1e-06
HIGH = lax.Precision.HIGHEST
MESH = pl.DeviceIdType.MESH
NX, NY, NZ, RANK = 4, 8, 8, 256
F32 = jnp.float32


def dot(a, b, ca=1, cb=0):
    return lax.dot_general(
        a, b, (((ca,), (cb,)), ((), ())), precision=HIGH, preferred_element_type=F32
    )


def halves(v):
    high = v.astype(jnp.bfloat16)
    return high, (v - high.astype(F32)).astype(jnp.bfloat16)


def dot_halves(a, b, ca=1, cb=0):
    dims = (((ca,), (cb,)), ((), ()))

    def one(u, v):
        return lax.dot_general(u, v, dims, preferred_element_type=F32)

    return one(a[0], b[0]) + (one(a[0], b[1]) + one(a[1], b[0]))


def invert_half(a, hook=None):
    lanes = lax.broadcasted_iota(jnp.int32, (8, 128), 1)
    subs = lax.broadcasted_iota(jnp.int32, (8, 128), 0)
    groups = [a[8 * g : 8 * g + 8] for g in range(16)]
    done = []
    for k in range(16):
        base = 8 * k
        inside = (lanes >= base) & (lanes < base + 8)
        panel = groups[0]
        cols = [jnp.broadcast_to(panel[:, base + j : base + j + 1], (8, 128)) for j in range(8)]
        held = jnp.where(inside, (lanes == subs + base).astype(F32), panel)
        pivots = cols[0]
        inverse, heads = [], []
        for j in range(8):
            r = 1.0 / cols[j][j : j + 1]
            inverse.append(r)
            mult = jnp.where(subs > j, cols[j] * r, 0.0)
            heads.append([c[j : j + 1] for c in cols])
            for jj in range(j + 1, 8):
                cols[jj] = cols[jj] - mult * heads[j][jj]
            held = held - mult * held[j : j + 1]
            if j:
                pivots = jnp.where(subs == j, cols[j], pivots)
        done.append(jnp.where(lanes <= subs + base, held * lax.rsqrt(pivots), 0.0))
        rest = []
        for g in groups[1:]:
            c = [jnp.broadcast_to(g[:, base + j : base + j + 1], (8, 128)) for j in range(8)]
            out = jnp.where(inside, 0.0, g)
            for j in range(8):
                m = c[j] * inverse[j]
                for jj in range(j + 1, 8):
                    c[jj] = c[jj] - m * heads[j][jj]
                out = out - m * held[j : j + 1]
            rest.append(out)
        groups = rest
        if hook is not None:
            hook(k)
    return jnp.concatenate(done, axis=0)


def place():
    f = lax.axis_index("fsdp")
    return f // 16, lax.rem(f // 2, 8), lax.rem(f, 2), lax.axis_index("tp")


NEAR_FIRST = (1, 7, 2, 6, 3, 5, 4)
FAR_FIRST = (4, 3, 5, 2, 6, 1, 7)


def kernel(
    mom_up, grad_up, basis_up, mom_down, grad_down, basis_down,
    upd_up, new_up, nb_up, upd_down, new_down, nb_down,
    q, wfull, wpart, wcore, wsum, wu_x, wu_s, wu_y, wd_y, wd_s, wd_x,
    m_up, m_down, blend_up, blend_down, r_up, o_upd_up, o_new_up, o_upd_down, o_new_down,
    part_up, part_up_in, pfull_up, part_down, part_down_in, pfull_down,
    gram, gram_in, gsum, g_x, g_xs, g_y, g_all, xinv, ssum, ssum_in,
    g_up, g_down, bu_hi, bu_lo, pd_hi, pd_lo, tu_hi, tu_lo, td_hi, td_lo,
    send, recv, local,
):
    x, y, c, z = place()
    count = [0]

    def at(xx, yy, cc, zz):
        return (xx * 16 + yy * 2 + cc, zz)

    def along_y(d):
        return at(x, lax.rem(y + d, NY), c, z)

    def along_x(d):
        return at(lax.rem(x + d, NX), y, c, z)

    def along_z(d):
        return at(x, y, c, lax.rem(z + d, NZ))

    sibling = at(x, y, 1 - c, z)

    barrier = pltpu.get_barrier_semaphore()
    peers = (
        [along_y(d) for d in range(1, NY)]
        + [along_x(d) for d in range(1, NX)]
        + [along_z(d) for d in range(1, NZ)]
        + [sibling]
    )
    for peer in peers:
        pl.semaphore_signal(barrier, inc=1, device_id=peer, device_id_type=MESH)
    loads = [
        pltpu.make_async_copy(src, dst, local.at[i])
        for i, (src, dst) in enumerate(
            ((mom_down, m_down), (grad_down, g_down), (mom_up, m_up), (grad_up, g_up))
        )
    ]
    for load in loads:
        load.start()

    started = []

    def transfer(src, dst, device, arrives):
        n = count[0]
        count[0] += 1
        copy = pltpu.make_async_remote_copy(
            src, dst, send.at[n], recv.at[n], device_id=device, device_id_type=MESH
        )
        copy.start()
        started.append(copy)
        landing = pltpu.make_async_remote_copy(
            src, arrives, send.at[n], recv.at[n], device_id=device, device_id_type=MESH
        )
        return landing.wait_recv

    def wait(waits):
        for w in waits:
            w()

    def back(v, d, n):
        return lax.rem(v + n - d, n)

    class Gather:
        def __init__(self, buf):
            self.buf = buf
            self.down_x = [
                transfer(buf.at[x, y, c, 24:32], buf.at[x, y, c, 24:32], along_x(d),
                         buf.at[back(x, d, NX), y, c, 24:32])
                for d in range(1, NX)
            ]
            self.up_y = {
                d: transfer(buf.at[x, y, c, 0:24], buf.at[x, y, c, 0:24], along_y(d),
                            buf.at[x, back(y, d, NY), c, 0:24])
                for d in NEAR_FIRST
            }
            self.up_x = {d: [] for d in range(1, NX)}
            self.forward(y)

        def forward(self, yy):
            for d in range(1, NX):
                piece = self.buf.at[x, yy, c, 0:24]
                self.up_x[d].append(
                    transfer(piece, piece, along_x(d), self.buf.at[back(x, d, NX), yy, c, 0:24])
                )

        def second(self):
            buf = self.buf
            wait(self.down_x)
            self.down_y = [
                transfer(buf.at[:, y, c, 24:32], buf.at[:, y, c, 24:32], along_y(d),
                         buf.at[:, back(y, d, NY), c, 24:32])
                for d in range(1, NY)
            ]
            for d in NEAR_FIRST:
                self.up_y[d]()
                self.forward(back(y, d, NY))
            self.cores = [self.across(x)]

        def across(self, xx):
            block = self.buf.at[xx, :, c, 0:24]
            return transfer(block, block, sibling, self.buf.at[xx, :, 1 - c, 0:24])

        def down(self):
            wait(self.down_y)
            block = self.buf.at[:, :, c, 24:32]
            transfer(block, block, sibling, self.buf.at[:, :, 1 - c, 24:32])()

        def up(self, use):
            for d in range(1, NX):
                wait(self.up_x[d])
                self.cores.append(self.across(back(x, d, NX)))
                self.cores[d - 1]()
                use(back(x, d - 1, NX))
            self.cores[NX - 1]()
            use(back(x, NX - 1, NX))

    q[x, y, c, 0:24, :] = basis_up[0]
    q[x, y, c, 24:32, :] = jnp.zeros((8, RANK), F32)
    for i in range(6):
        q[x, y, c, 24 + i : 25 + i, :] = basis_down[i]
    pl.semaphore_wait(barrier, len(peers))
    first = Gather(q)

    column = lax.broadcasted_iota(jnp.int32, (384, 512), 0)
    slot = lax.broadcasted_iota(jnp.int32, (384, 512), 1)
    pick = ((column == (slot // 8) * 6 + lax.rem(slot, 8)) & (lax.rem(slot, 8) < 6)).astype(F32)
    for load in loads:
        load.wait()
    blend_down[...] = m_down[...] + g_down[...].astype(F32)
    blend_up[...] = m_up[...] + g_up[...].astype(F32)
    for g in range(NX):
        bu_hi[g], bu_lo[g] = halves(blend_up[:, 384 * g : 384 * g + 384])
    padded = dot(blend_down[...], pick)
    pd_hi[...], pd_lo[...] = halves(padded)
    first.second()
    first.down()

    p_part = dot_halves(
        (pd_hi[...], pd_lo[...]), halves(q[:, :, :, 24:32, :].reshape(512, RANK))
    )
    part_down[...] = p_part.reshape(NZ, 24, RANK)

    def reduce_z(part, part_in):
        return [
            transfer(part.at[lax.rem(z + d, NZ)], part_in.at[d - 1], along_z(d), part_in.at[d - 1])
            for d in FAR_FIRST
        ]

    def gather_z(part, part_in, full):
        total = part[z]
        for d in range(1, NZ):
            total = total + part_in[d - 1]
        full[z] = total
        return [
            transfer(full.at[z], full.at[z], along_z(d), full.at[back(z, d, NZ)])
            for d in FAR_FIRST
        ]

    down_rs = reduce_z(part_down, part_down_in)
    sums_up = []

    def add_up(g):
        piece = halves(q[g, :, :, 0:24, :].reshape(384, RANK))
        sums_up.append(dot_halves((bu_hi[g], bu_lo[g]), piece))

    first.up(add_up)
    part_up[0:6] = (sums_up[0] + sums_up[1] + sums_up[2] + sums_up[3]).reshape(6, 8, RANK)
    part_up[6:8] = jnp.zeros((2, 8, RANK), F32)
    up_rs = reduce_z(part_up, part_up_in)
    for g in range(NX):
        tu_hi[g], tu_lo[g] = halves(blend_up[:, 384 * g : 384 * g + 384].T)
    td_hi[...], td_lo[...] = halves(padded.T)
    wait(down_rs)
    down_ag = gather_z(part_down, part_down_in, pfull_down)
    wait(up_rs)
    up_ag = gather_z(part_up, part_up_in, pfull_up)

    wait(down_ag)
    p_down = pfull_down[...].reshape(192, RANK)
    gram[1] = dot(p_down, p_down, 0, 0)
    wait(up_ag)
    p_up = pfull_up[0:6].reshape(48, RANK)
    gram[0] = dot(p_up, p_up, 0, 0)
    gram_wait = transfer(gram.at[1 - c], gram_in, sibling, gram_in)
    gram_wait()
    gsum[...] = (gram[c] + gram_in[...]).reshape(NX, 64, RANK)
    gram_x = [
        transfer(gsum.at[lax.rem(x + d, NX)], g_x.at[d - 1], along_x(d), g_x.at[d - 1])
        for d in (2, 1, 3)
    ]
    p_halves = halves(p_down)
    wpart[:, :, :, 24:32, :] = dot_halves((td_hi[...], td_lo[...]), p_halves).reshape(
        NX, NY, 2, 8, RANK
    )
    core_down = transfer(
        wpart.at[:, :, 1 - c, 24:32], wcore.at[:, :, 24:32], sibling, wcore.at[:, :, 24:32]
    )
    p_halves = halves(p_up)
    for g in range(NX):
        wpart[g, :, :, 0:24, :] = dot_halves((tu_hi[g], tu_lo[g]), p_halves).reshape(
            NY, 2, 24, RANK
        )
    core_up = transfer(
        wpart.at[:, :, 1 - c, 0:24], wcore.at[:, :, 0:24], sibling, wcore.at[:, :, 0:24]
    )
    wait(gram_x)
    g_xs[...] = (gsum[x] + g_x[0] + g_x[1] + g_x[2]).reshape(NY, 8, RANK)
    gram_y = [
        transfer(g_xs.at[lax.rem(y + d, NY)], g_y.at[d - 1], along_y(d), g_y.at[d - 1])
        for d in FAR_FIRST
    ]
    core_down()
    core_up()
    wsum[...] = wpart[:, :, c] + wcore[...]
    w_x = {}

    def scatter_x(d):
        yy = lax.rem(y + d, NY)
        w_x[d] = [
            transfer(wsum.at[lax.rem(x + e, NX), yy, 0:24], wu_x.at[e - 1, d], along_x(e),
                     wu_x.at[e - 1, d])
            for e in (2, 1, 3)
        ]

    w_y = []

    def scatter_y(d):
        wait(w_x[d])
        wu_s[d] = wsum[x, lax.rem(y + d, NY), 0:24] + wu_x[0, d] + wu_x[1, d] + wu_x[2, d]
        if d:
            w_y.append(transfer(wu_s.at[d], wu_y.at[d - 1], along_y(d), wu_y.at[d - 1]))

    for d in (4, 3, 5, 2):
        scatter_x(d)
    wait(gram_y)
    row = g_xs[y]
    for d in range(1, NY):
        row = row + g_y[d - 1]
    g_all[x, y] = row
    gram_y = [
        transfer(g_all.at[x, y], g_all.at[x, y], along_y(d), g_all.at[x, back(y, d, NY)])
        for d in FAR_FIRST
    ]
    down_y = [
        transfer(wsum.at[:, lax.rem(y + d, NY), 24:32], wd_y.at[d - 1], along_y(d), wd_y.at[d - 1])
        for d in FAR_FIRST
    ]
    wait(gram_y)
    gram_x = [
        transfer(g_all.at[x], g_all.at[x], along_x(d), g_all.at[back(x, d, NX)])
        for d in (2, 1, 3)
    ]
    for d in (6, 1, 7, 0):
        scatter_x(d)
    for d in (4, 3, 5, 2):
        scatter_y(d)
    wait(gram_x)

    g11, g12, g22 = (
        g_all[0:2, :, :, 0:128].reshape(128, 128),
        g_all[0:2, :, :, 128:256].reshape(128, 128),
        g_all[2:4, :, :, 128:256].reshape(128, 128),
    )
    down_x = []

    def scatter_down():
        wait(down_y)
        owned = wsum[:, y, 24:32]
        for d in range(1, NY):
            owned = owned + wd_y[d - 1]
        wd_s[...] = owned
        down_x.extend(
            transfer(wd_s.at[lax.rem(x + d, NX)], wd_x.at[d - 1], along_x(d), wd_x.at[d - 1])
            for d in (2, 1, 3)
        )

    def hook(k):
        if k == 3:
            scatter_y(6)
        if k == 5:
            scatter_down()
        if k == 7:
            scatter_y(1)
            scatter_y(7)
        if k == 9:
            scatter_y(0)

    x11 = invert_half(g11, hook)
    xinv[c, 0:128, 0:128] = x11
    xinv[c, 0:128, 128:256] = jnp.zeros((128, 128), F32)
    u = dot(x11, g12)
    low = g22 - dot(u, u, 0, 0)
    corner = dot(u, x11, 0, 0)
    gathers = []

    def hook(k):
        if k == 5:
            wait(w_y)
            owned = wu_s[0]
            for d in range(1, NY):
                owned = owned + wu_y[d - 1]
            wfull[x, y, c, 0:24, :] = owned
            wait(down_x)
            wfull[x, y, c, 24:32, :] = wd_s[x] + wd_x[0] + wd_x[1] + wd_x[2]
            gathers.append(Gather(wfull))
        if k == 13:
            gathers[0].second()

    x22 = invert_half(low, hook)
    xinv[c, 128:256, 128:256] = x22
    xinv[c, 128:256, 0:128] = -dot(x22, corner)
    x_wait = transfer(xinv.at[c], xinv.at[c], sibling, xinv.at[1 - c])
    x_wait()
    o_up = dot(p_up, xinv[0], 1, 1)
    o_down = dot(p_down, xinv[1], 1, 1)
    x_up, x_down = halves(xinv[0]), halves(xinv[1])
    ou_halves, od_halves = halves(o_up), halves(o_down)

    last = gathers[0]
    last.down()
    right_down = dot_halves(
        halves(dot(pick, wfull[:, :, :, 24:32, :].reshape(512, RANK))), x_down, 1, 1
    )
    rd_halves = halves(right_down)
    o_new_down[...] = blend_down[...] - (1.0 - retain) * dot_halves(od_halves, rd_halves, 1, 1)
    writes = []

    def write(src, dst):
        copy = pltpu.make_async_copy(src, dst, local.at[4 + len(writes)])
        copy.start()
        writes.append(copy)

    write(o_new_down, new_down)
    squares = []

    def turn(g):
        right = dot_halves(halves(wfull[g, :, :, 0:24, :].reshape(384, RANK)), x_up, 1, 1)
        r_up[g] = right
        squares.append(jnp.sum(right * right, axis=0, keepdims=True))

    last.up(turn)
    ssum[...] = jnp.zeros((8, RANK), F32)
    ssum[0:1, :] = squares[0] + squares[1] + squares[2] + squares[3]
    ssum[1:2, :] = jnp.sum(right_down * right_down, axis=0, keepdims=True)
    s_wait = [
        transfer(ssum, ssum_in.at[d - 1], along_z(d), ssum_in.at[d - 1]) for d in FAR_FIRST
    ]
    ru_halves = [halves(r_up[g]) for g in range(NX)]
    for g in range(NX):
        cols = slice(384 * g, 384 * g + 384)
        o_new_up[:, cols] = blend_up[:, cols] - (1.0 - retain) * dot_halves(
            ou_halves, ru_halves[g], 1, 1
        )
    write(o_new_up, new_up)
    wait(s_wait)
    sums = ssum[...]
    for d in range(1, NZ):
        sums = sums + ssum_in[d - 1]
    scale = lax.rsqrt(sums + epsilon)
    s_up, s_down = scale[0:1], scale[1:2]
    ou_halves = halves(math.sqrt(3072 / 12288) * o_up * s_up)
    for g in range(NX):
        o_upd_up[:, 384 * g : 384 * g + 384] = dot_halves(ou_halves, ru_halves[g], 1, 1)
    write(o_upd_up, upd_up)
    od_halves = halves(math.sqrt(12288 / 3072) * o_down * s_down)
    o_upd_down[...] = dot_halves(od_halves, rd_halves, 1, 1)
    write(o_upd_down, upd_down)
    nb_up[0] = dot(wfull[x, y, c, 0:24, :], xinv[0], 1, 1) * s_up
    nb = dot(wfull[x, y, c, 24:32, :], xinv[1], 1, 1) * s_down
    for i in range(6):
        nb_down[i] = nb[i : i + 1]
    for copy in started:
        copy.wait_send()
    for copy in writes:
        copy.wait()


PIECES = (NX, NY, 2, 32, RANK)
SCRATCH = (
    [PIECES, PIECES, PIECES, (NX, NY, 32, RANK), (NX, NY, 32, RANK)]
    + [(NX - 1, NY, 24, RANK), (NY, 24, RANK), (NY - 1, 24, RANK)]
    + [(NY - 1, NX, 8, RANK), (NX, 8, RANK), (NX - 1, 8, RANK)]
    + [(48, 1536), (192, 384), (48, 1536), (192, 384), (NX, 384, RANK)]
    + [(48, 1536), (48, 1536), (192, 384), (192, 384)]
    + [(NZ, 8, RANK), (NZ - 1, 8, RANK), (NZ, 8, RANK)]
    + [(NZ, 24, RANK), (NZ - 1, 24, RANK), (NZ, 24, RANK)]
    + [(2, RANK, RANK), (RANK, RANK), (NX, 64, RANK), (NX - 1, 64, RANK), (NY, 8, RANK)]
    + [(NY - 1, 8, RANK), (NX, NY, 8, RANK)]
    + [(2, RANK, RANK), (8, RANK), (NZ - 1, 8, RANK)]
)
HALF_SCRATCH = (
    [(48, 1536), (192, 384)]
    + [(NX, 48, 384)] * 2
    + [(192, 512)] * 2
    + [(NX, 384, 48)] * 2
    + [(512, 192)] * 2
)
COPIES = 224


def finish(*refs):
    sources, results, sems = refs[0:6], refs[6:12], refs[12]
    copies = [
        pltpu.make_async_copy(src, dst, sems.at[i])
        for i, (src, dst) in enumerate(zip(sources, results))
    ]
    for copy in copies:
        copy.start()
    for copy in copies:
        copy.wait()


def body(mom_up, grad_up, basis_up, mom_down, grad_down, basis_down):
    vmem = pl.BlockSpec(memory_space=pltpu.VMEM)
    anywhere = pl.BlockSpec(memory_space=pl.ANY)
    shapes = [(48, 1536), (48, 1536), (1, 24, RANK), (192, 384), (192, 384), (6, 1, RANK)]
    out_shape = [jax.ShapeDtypeStruct(s, F32) for s in shapes]
    results = pl.pallas_call(
        kernel,
        out_shape=out_shape,
        in_specs=[anywhere, anywhere, vmem] * 2,
        out_specs=[anywhere, anywhere, vmem] * 2,
        scratch_shapes=[pltpu.VMEM(s, F32) for s in SCRATCH]
        + [pltpu.VMEM(s, jnp.bfloat16) for s in HALF_SCRATCH]
        + [pltpu.SemaphoreType.DMA((COPIES,))] * 2
        + [pltpu.SemaphoreType.DMA((8,))],
        compiler_params=pltpu.CompilerParams(
            collective_id=0, has_side_effects=True, vmem_limit_bytes=60 << 20
        ),
    )(mom_up, grad_up, basis_up, mom_down, grad_down, jnp.swapaxes(basis_down, 0, 1))
    results = pl.pallas_call(
        finish,
        out_shape=out_shape,
        in_specs=[anywhere] * 6,
        out_specs=[anywhere] * 6,
        scratch_shapes=[pltpu.SemaphoreType.DMA((6,))],
    )(*results)
    return (*results[:5], jnp.swapaxes(results[5], 0, 1))


def solution(mesh):
    specs = (P("fsdp", "tp"), P("fsdp", "tp"), P("tp", "fsdp", None)) * 2
    return jax.shard_map(
        body,
        mesh=mesh,
        in_specs=specs,
        out_specs=specs,
        check_vma=False,
    )
```

```python
import math

import jax
import jax.numpy as jnp
from jax import lax
from jax.experimental import pallas as pl
from jax.experimental.pallas import tpu as pltpu
from jax.sharding import PartitionSpec as P

retain = 0.9
epsilon = 1e-06
HIGH = lax.Precision.HIGHEST
MESH = pl.DeviceIdType.MESH
NX, NY, NZ, RANK = 4, 8, 8, 256
F32 = jnp.float32


def dot(a, b, ca=1, cb=0):
    return lax.dot_general(
        a, b, (((ca,), (cb,)), ((), ())), precision=HIGH, preferred_element_type=F32
    )


def halves(v):
    high = v.astype(jnp.bfloat16)
    return high, (v - high.astype(F32)).astype(jnp.bfloat16)


def dot_halves(a, b, ca=1, cb=0):
    dims = (((ca,), (cb,)), ((), ()))

    def one(u, v):
        return lax.dot_general(u, v, dims, preferred_element_type=F32)

    return one(a[0], b[0]) + (one(a[0], b[1]) + one(a[1], b[0]))


def invert_half(a, hook=None):
    lanes = lax.broadcasted_iota(jnp.int32, (8, 128), 1)
    subs = lax.broadcasted_iota(jnp.int32, (8, 128), 0)
    groups = [a[8 * g : 8 * g + 8] for g in range(16)]
    done = []
    for k in range(16):
        base = 8 * k
        inside = (lanes >= base) & (lanes < base + 8)
        panel = groups[0]
        cols = [jnp.broadcast_to(panel[:, base + j : base + j + 1], (8, 128)) for j in range(8)]
        held = jnp.where(inside, (lanes == subs + base).astype(F32), panel)
        pivots = cols[0]
        inverse, heads = [], []
        for j in range(8):
            r = 1.0 / cols[j][j : j + 1]
            inverse.append(r)
            mult = jnp.where(subs > j, cols[j] * r, 0.0)
            heads.append([c[j : j + 1] for c in cols])
            for jj in range(j + 1, 8):
                cols[jj] = cols[jj] - mult * heads[j][jj]
            held = held - mult * held[j : j + 1]
            if j:
                pivots = jnp.where(subs == j, cols[j], pivots)
        done.append(jnp.where(lanes <= subs + base, held * lax.rsqrt(pivots), 0.0))
        rest = []
        for g in groups[1:]:
            c = [jnp.broadcast_to(g[:, base + j : base + j + 1], (8, 128)) for j in range(8)]
            out = jnp.where(inside, 0.0, g)
            for j in range(8):
                m = c[j] * inverse[j]
                for jj in range(j + 1, 8):
                    c[jj] = c[jj] - m * heads[j][jj]
                out = out - m * held[j : j + 1]
            rest.append(out)
        groups = rest
        if hook is not None:
            hook(k)
    return jnp.concatenate(done, axis=0)


def place():
    f = lax.axis_index("fsdp")
    return f // 16, lax.rem(f // 2, 8), lax.rem(f, 2), lax.axis_index("tp")


NEAR_FIRST = (1, 7, 2, 6, 3, 5, 4)
FAR_FIRST = (4, 3, 5, 2, 6, 1, 7)


def kernel(
    mom_up, grad_up, basis_up, mom_down, grad_down, basis_down,
    upd_up, new_up, nb_up, upd_down, new_down, nb_down,
    q, wfull, wpart, wcore, wsum, wu_x, wu_s, wu_y, wd_y, wd_s, wd_x,
    m_up, m_down, blend_up, blend_down, r_up, o_upd_up, o_new_up, o_upd_down, o_new_down,
    part_up, part_up_in, pfull_up, part_down, part_down_in, pfull_down,
    gram, gram_in, gsum, g_x, g_y, g_all, xinv, ssum, ssum_in,
    g_up, g_down, bu_hi, bu_lo, pd_hi, pd_lo, tu_hi, tu_lo, td_hi, td_lo,
    send, recv, local,
):
    x, y, c, z = place()
    count = [0]

    def at(xx, yy, cc, zz):
        return (xx * 16 + yy * 2 + cc, zz)

    def along_y(d):
        return at(x, lax.rem(y + d, NY), c, z)

    def along_x(d):
        return at(lax.rem(x + d, NX), y, c, z)

    def along_z(d):
        return at(x, y, c, lax.rem(z + d, NZ))

    sibling = at(x, y, 1 - c, z)

    barrier = pltpu.get_barrier_semaphore()
    peers = (
        [along_y(d) for d in range(1, NY)]
        + [along_x(d) for d in range(1, NX)]
        + [along_z(d) for d in range(1, NZ)]
        + [sibling]
    )
    for peer in peers:
        pl.semaphore_signal(barrier, inc=1, device_id=peer, device_id_type=MESH)
    loads = [
        pltpu.make_async_copy(src, dst, local.at[i])
        for i, (src, dst) in enumerate(
            ((mom_down, m_down), (grad_down, g_down), (mom_up, m_up), (grad_up, g_up))
        )
    ]
    for load in loads:
        load.start()

    started = []

    def transfer(src, dst, device, arrives):
        n = count[0]
        count[0] += 1
        copy = pltpu.make_async_remote_copy(
            src, dst, send.at[n], recv.at[n], device_id=device, device_id_type=MESH
        )
        copy.start()
        started.append(copy)
        landing = pltpu.make_async_remote_copy(
            src, arrives, send.at[n], recv.at[n], device_id=device, device_id_type=MESH
        )
        return landing.wait_recv

    def wait(waits):
        for w in waits:
            w()

    def back(v, d, n):
        return lax.rem(v + n - d, n)

    class Gather:
        def __init__(self, buf):
            self.buf = buf
            self.down_x = [
                transfer(buf.at[x, y, c, 24:32], buf.at[x, y, c, 24:32], along_x(d),
                         buf.at[back(x, d, NX), y, c, 24:32])
                for d in range(1, NX)
            ]
            self.up_y = {
                d: transfer(buf.at[x, y, c, 0:24], buf.at[x, y, c, 0:24], along_y(d),
                            buf.at[x, back(y, d, NY), c, 0:24])
                for d in NEAR_FIRST
            }
            self.up_x = {d: [] for d in range(1, NX)}
            self.forward(y)

        def forward(self, yy):
            for d in (2, 1, 3):
                piece = self.buf.at[x, yy, c, 0:24]
                self.up_x[d].append(
                    transfer(piece, piece, along_x(d), self.buf.at[back(x, d, NX), yy, c, 0:24])
                )

        def turn(self):
            buf = self.buf
            wait(self.down_x)
            self.down_y = [
                transfer(buf.at[:, y, c, 24:32], buf.at[:, y, c, 24:32], along_y(d),
                         buf.at[:, back(y, d, NY), c, 24:32])
                for d in FAR_FIRST
            ]

        def relay(self, *steps):
            for d in steps:
                self.up_y[d]()
                self.forward(back(y, d, NY))

        def own(self):
            self.cores = {0: self.across(x)}

        def column(self, d):
            wait(self.up_x[d])
            self.cores[d] = self.across(back(x, d, NX))

        def second(self):
            self.turn()
            self.relay(*NEAR_FIRST)
            self.own()

        def across(self, xx):
            block = self.buf.at[xx, :, c, 0:24]
            return transfer(block, block, sibling, self.buf.at[xx, :, 1 - c, 0:24])

        def down(self):
            wait(self.down_y)
            block = self.buf.at[:, :, c, 24:32]
            return transfer(block, block, sibling, self.buf.at[:, :, 1 - c, 24:32])

        def up(self, use):
            before = 0
            for d in (1, 3, 2):
                if d not in self.cores:
                    self.column(d)
                self.cores[before]()
                use(back(x, before, NX))
                before = d
            self.cores[before]()
            use(back(x, before, NX))

    q[x, y, c, 0:24, :] = basis_up[0]
    q[x, y, c, 24:32, :] = jnp.zeros((8, RANK), F32)
    for i in range(6):
        q[x, y, c, 24 + i : 25 + i, :] = basis_down[i]
    pl.semaphore_wait(barrier, len(peers))
    first = Gather(q)

    column = lax.broadcasted_iota(jnp.int32, (384, 512), 0)
    slot = lax.broadcasted_iota(jnp.int32, (384, 512), 1)
    pick = ((column == (slot // 8) * 6 + lax.rem(slot, 8)) & (lax.rem(slot, 8) < 6)).astype(F32)
    for load in loads:
        load.wait()
    blend_down[...] = m_down[...] + g_down[...].astype(F32)
    blend_up[...] = m_up[...] + g_up[...].astype(F32)
    for g in range(NX):
        bu_hi[g], bu_lo[g] = halves(blend_up[:, 384 * g : 384 * g + 384])
    padded = dot(blend_down[...], pick)
    pd_hi[...], pd_lo[...] = halves(padded)
    first.second()
    first.down()()

    p_part = dot_halves(
        (pd_hi[...], pd_lo[...]), halves(q[:, :, :, 24:32, :].reshape(512, RANK))
    )
    part_down[...] = p_part.reshape(NZ, 24, RANK)

    def reduce_z(part, part_in):
        return [
            transfer(part.at[lax.rem(z + d, NZ)], part_in.at[d - 1], along_z(d), part_in.at[d - 1])
            for d in FAR_FIRST
        ]

    def gather_z(part, part_in, full):
        total = part[z]
        for d in range(1, NZ):
            total = total + part_in[d - 1]
        full[z] = total
        return [
            transfer(full.at[z], full.at[z], along_z(d), full.at[back(z, d, NZ)])
            for d in FAR_FIRST
        ]

    down_rs = reduce_z(part_down, part_down_in)
    sums_up = []

    def add_up(g):
        piece = halves(q[g, :, :, 0:24, :].reshape(384, RANK))
        sums_up.append(dot_halves((bu_hi[g], bu_lo[g]), piece))

    first.up(add_up)
    part_up[0:6] = (sums_up[0] + sums_up[1] + sums_up[2] + sums_up[3]).reshape(6, 8, RANK)
    part_up[6:8] = jnp.zeros((2, 8, RANK), F32)
    up_rs = reduce_z(part_up, part_up_in)
    for g in range(NX):
        tu_hi[g], tu_lo[g] = halves(blend_up[:, 384 * g : 384 * g + 384].T)
    td_hi[...], td_lo[...] = halves(padded.T)
    wait(down_rs)
    down_ag = gather_z(part_down, part_down_in, pfull_down)
    wait(up_rs)
    up_ag = gather_z(part_up, part_up_in, pfull_up)

    wait(down_ag)
    p_down = pfull_down[...].reshape(192, RANK)
    gram[1] = dot(p_down, p_down, 0, 0).reshape(NZ, 32, RANK)
    wait(up_ag)
    p_up = pfull_up[0:6].reshape(48, RANK)
    gram[0] = dot(p_up, p_up, 0, 0).reshape(NZ, 32, RANK)
    gram_wait = transfer(gram.at[1 - c, z], gram_in, sibling, gram_in)
    p_halves = halves(p_up)
    core_up = {}

    def multiply(e):
        g = lax.rem(x + e, NX)
        wpart[g, :, :, 0:24, :] = dot_halves((tu_hi[g], tu_lo[g]), p_halves).reshape(
            NY, 2, 24, RANK
        )
        core_up[e] = transfer(
            wpart.at[g, :, 1 - c, 0:24], wcore.at[g, :, 0:24], sibling, wcore.at[g, :, 0:24]
        )

    def join(e):
        g = lax.rem(x + e, NX)
        core_up[e]()
        wsum[g, :, 0:24] = wpart[g, :, c, 0:24] + wcore[g, :, 0:24]

    w_x = {d: [] for d in range(NY)}

    def scatter_x(e, d):
        yy = lax.rem(y + d, NY)
        w_x[d].append(
            transfer(wsum.at[lax.rem(x + e, NX), yy, 0:24], wu_x.at[e - 1, d], along_x(e),
                     wu_x.at[e - 1, d])
        )

    w_y = []

    def scatter_y(d):
        wait(w_x[d])
        wu_s[d] = wsum[x, lax.rem(y + d, NY), 0:24] + wu_x[0, d] + wu_x[1, d] + wu_x[2, d]
        if d:
            w_y.append(transfer(wu_s.at[d], wu_y.at[d - 1], along_y(d), wu_y.at[d - 1]))

    multiply(2)
    gram_wait()
    gsum[...] = (gram[c, z] + gram_in[...]).reshape(NX, 8, RANK)
    gram_x = [
        transfer(gsum.at[lax.rem(x + d, NX)], g_x.at[d - 1], along_x(d), g_x.at[d - 1])
        for d in (2, 1, 3)
    ]
    multiply(1)
    multiply(3)
    join(2)
    for d in FAR_FIRST + (0,):
        scatter_x(2, d)
    wait(gram_x)
    g_y[y] = gsum[x] + g_x[0] + g_x[1] + g_x[2]
    gram_y = [
        transfer(g_y.at[y], g_y.at[y], along_y(d), g_y.at[back(y, d, NY)]) for d in FAR_FIRST
    ]
    wpart[:, :, :, 24:32, :] = dot_halves((td_hi[...], td_lo[...]), halves(p_down)).reshape(
        NX, NY, 2, 8, RANK
    )
    core_down = transfer(
        wpart.at[:, :, 1 - c, 24:32], wcore.at[:, :, 24:32], sibling, wcore.at[:, :, 24:32]
    )
    join(1)
    join(3)
    for d in FAR_FIRST + (0,):
        scatter_x(1, d)
        scatter_x(3, d)
    multiply(0)
    core_down()
    wsum[:, :, 24:32] = wpart[:, :, c, 24:32] + wcore[:, :, 24:32]
    down_y = [
        transfer(wsum.at[:, lax.rem(y + d, NY), 24:32], wd_y.at[d - 1], along_y(d), wd_y.at[d - 1])
        for d in FAR_FIRST
    ]
    join(0)
    wait(gram_y)
    row = g_y[0]
    for i in range(1, NY):
        row = row + g_y[i]
    g_all[z, x] = row
    gram_z = [
        transfer(g_all.at[z, x], g_all.at[z, x], along_z(d), g_all.at[back(z, d, NZ), x])
        for d in FAR_FIRST
    ]
    for d in FAR_FIRST[:3]:
        scatter_y(d)
    wait(gram_z)
    gram_x = []
    for d in (2, 1, 3):
        xx = back(x, d, NX)
        gram_x.append(transfer(g_all.at[0:4, x], g_all.at[0:4, x], along_x(d), g_all.at[0:4, xx]))
        gram_x.append(
            transfer(g_all.at[4:8, x, :, 128:256], g_all.at[4:8, x, :, 128:256], along_x(d),
                     g_all.at[4:8, xx, :, 128:256])
        )
    for d in FAR_FIRST[3:]:
        scatter_y(d)
    wait(down_y)
    owned = wsum[:, y, 24:32]
    for d in range(1, NY):
        owned = owned + wd_y[d - 1]
    wd_s[...] = owned
    down_x = [
        transfer(wd_s.at[lax.rem(x + d, NX)], wd_x.at[d - 1], along_x(d), wd_x.at[d - 1])
        for d in (2, 1, 3)
    ]
    scatter_y(0)
    wait(w_y)
    owned = wu_s[0]
    for d in range(1, NY):
        owned = owned + wu_y[d - 1]
    wfull[x, y, c, 0:24, :] = owned
    wait(down_x)
    wfull[x, y, c, 24:32, :] = wd_s[x] + wd_x[0] + wd_x[1] + wd_x[2]
    last = Gather(wfull)
    wait(gram_x)

    g11, g12, g22 = (
        g_all[0:4, :, :, 0:128].reshape(128, 128),
        g_all[0:4, :, :, 128:256].reshape(128, 128),
        g_all[4:8, :, :, 128:256].reshape(128, 128),
    )

    def hook(k):
        if k == 1:
            last.relay(1, 7)
            last.turn()
        if k == 5:
            last.relay(2, 6)
        if k == 9:
            last.relay(3, 5)
        if k == 12:
            last.relay(4)
            last.own()

    x11 = invert_half(g11, hook)
    xinv[c, 0:128, 0:128] = x11
    xinv[c, 0:128, 128:256] = jnp.zeros((128, 128), F32)
    u = dot(x11, g12)
    low = g22 - dot(u, u, 0, 0)
    corner = dot(u, x11, 0, 0)

    late = []

    def hook(k):
        if k == 6:
            late.append(last.down())
        if k == 9:
            last.column(1)
        if k == 11:
            late[0]()
            late.append(halves(dot(pick, wfull[:, :, :, 24:32, :].reshape(512, RANK))))
        if k == 12:
            last.column(3)

    x22 = invert_half(low, hook)
    xinv[c, 128:256, 128:256] = x22
    xinv[c, 128:256, 0:128] = -dot(x22, corner)
    x_wait = transfer(xinv.at[c], xinv.at[c], sibling, xinv.at[1 - c])
    x_wait()
    x_up, x_down = halves(xinv[0]), halves(xinv[1])

    right_down = dot_halves(late[1], x_down, 1, 1)
    squares = []

    def turn(g):
        right = dot_halves(halves(wfull[g, :, :, 0:24, :].reshape(384, RANK)), x_up, 1, 1)
        r_up[g] = right
        squares.append(jnp.sum(right * right, axis=0, keepdims=True))

    last.up(turn)
    ssum[...] = jnp.zeros((8, RANK), F32)
    ssum[0:1, :] = squares[0] + squares[1] + squares[2] + squares[3]
    ssum[1:2, :] = jnp.sum(right_down * right_down, axis=0, keepdims=True)
    s_wait = [
        transfer(ssum, ssum_in.at[d - 1], along_z(d), ssum_in.at[d - 1]) for d in FAR_FIRST
    ]
    o_up = dot_halves(halves(p_up), x_up, 1, 1)
    o_down = dot_halves(halves(p_down), x_down, 1, 1)
    ou_halves, od_halves = halves(o_up), halves(o_down)
    rd_halves = halves(right_down)
    writes = []

    def write(src, dst):
        copy = pltpu.make_async_copy(src, dst, local.at[4 + len(writes)])
        copy.start()
        writes.append(copy)

    o_new_down[...] = blend_down[...] - (1.0 - retain) * dot_halves(od_halves, rd_halves, 1, 1)
    write(o_new_down, new_down)
    ru_halves = [halves(r_up[g]) for g in range(NX)]
    for g in range(NX):
        cols = slice(384 * g, 384 * g + 384)
        o_new_up[:, cols] = blend_up[:, cols] - (1.0 - retain) * dot_halves(
            ou_halves, ru_halves[g], 1, 1
        )
    write(o_new_up, new_up)
    nb = dot_halves(halves(wfull[x, y, c, 24:32, :]), x_down, 1, 1)
    while started:
        started.pop().wait_send()
    wait(s_wait)
    sums = ssum[...]
    for d in range(1, NZ):
        sums = sums + ssum_in[d - 1]
    scale = lax.rsqrt(sums + epsilon)
    s_up, s_down = scale[0:1], scale[1:2]
    ou_halves = halves(math.sqrt(3072 / 12288) * o_up * s_up)
    for g in range(NX):
        o_upd_up[:, 384 * g : 384 * g + 384] = dot_halves(ou_halves, ru_halves[g], 1, 1)
    write(o_upd_up, upd_up)
    od_halves = halves(math.sqrt(12288 / 3072) * o_down * s_down)
    o_upd_down[...] = dot_halves(od_halves, rd_halves, 1, 1)
    write(o_upd_down, upd_down)
    nb_up[0] = r_up[x, pl.ds(pl.multiple_of(48 * y + 24 * c, 8), 24), :] * s_up
    nb = nb * s_down
    for i in range(6):
        nb_down[i] = nb[i : i + 1]
    for copy in writes:
        copy.wait()


PIECES = (NX, NY, 2, 32, RANK)
SCRATCH = (
    [PIECES, PIECES, PIECES, (NX, NY, 32, RANK), (NX, NY, 32, RANK)]
    + [(NX - 1, NY, 24, RANK), (NY, 24, RANK), (NY - 1, 24, RANK)]
    + [(NY - 1, NX, 8, RANK), (NX, 8, RANK), (NX - 1, 8, RANK)]
    + [(48, 1536), (192, 384), (48, 1536), (192, 384), (NX, 384, RANK)]
    + [(48, 1536), (48, 1536), (192, 384), (192, 384)]
    + [(NZ, 8, RANK), (NZ - 1, 8, RANK), (NZ, 8, RANK)]
    + [(NZ, 24, RANK), (NZ - 1, 24, RANK), (NZ, 24, RANK)]
    + [(2, NZ, 32, RANK), (32, RANK), (NX, 8, RANK), (NX - 1, 8, RANK), (NY, 8, RANK)]
    + [(NZ, NX, 8, RANK)]
    + [(2, RANK, RANK), (8, RANK), (NZ - 1, 8, RANK)]
)
HALF_SCRATCH = (
    [(48, 1536), (192, 384)]
    + [(NX, 48, 384)] * 2
    + [(192, 512)] * 2
    + [(NX, 384, 48)] * 2
    + [(512, 192)] * 2
)
COPIES = 232


def finish(*refs):
    sources, results, held, sems = refs[0:6], refs[6:12], refs[12:18], refs[18]
    reads = [pltpu.make_async_copy(a, b, sems.at[0, i]) for i, (a, b) in enumerate(zip(sources, held))]
    writes = [pltpu.make_async_copy(a, b, sems.at[1, i]) for i, (a, b) in enumerate(zip(held, results))]
    for copy in reads:
        copy.start()
    for read, write in zip(reads, writes):
        read.wait()
        write.start()
    for copy in writes:
        copy.wait()


def body(mom_up, grad_up, basis_up, mom_down, grad_down, basis_down):
    vmem = pl.BlockSpec(memory_space=pltpu.VMEM)
    anywhere = pl.BlockSpec(memory_space=pl.ANY)
    shapes = [(48, 1536), (48, 1536), (1, 24, RANK), (192, 384), (192, 384), (6, 1, RANK)]
    out_shape = [jax.ShapeDtypeStruct(s, F32) for s in shapes]
    results = pl.pallas_call(
        kernel,
        out_shape=out_shape,
        in_specs=[anywhere, anywhere, vmem] * 2,
        out_specs=[anywhere, anywhere, vmem] * 2,
        scratch_shapes=[pltpu.VMEM(s, F32) for s in SCRATCH]
        + [pltpu.VMEM(s, jnp.bfloat16) for s in HALF_SCRATCH]
        + [pltpu.SemaphoreType.DMA((COPIES,))] * 2
        + [pltpu.SemaphoreType.DMA((8,))],
        compiler_params=pltpu.CompilerParams(
            collective_id=0, has_side_effects=True, vmem_limit_bytes=60 << 20
        ),
    )(mom_up, grad_up, basis_up, mom_down, grad_down, jnp.swapaxes(basis_down, 0, 1))
    results = pl.pallas_call(
        finish,
        out_shape=out_shape,
        in_specs=[anywhere] * 6,
        out_specs=[anywhere] * 6,
        scratch_shapes=[pltpu.VMEM(s, F32) for s in shapes] + [pltpu.SemaphoreType.DMA((2, 6))],
    )(*results)
    return (*results[:5], jnp.swapaxes(results[5], 0, 1))


def solution(mesh):
    specs = (P("fsdp", "tp"), P("fsdp", "tp"), P("tp", "fsdp", None)) * 2
    return jax.shard_map(
        body,
        mesh=mesh,
        in_specs=specs,
        out_specs=specs,
        check_vma=False,
    )
```

```python
import math

import jax
import jax.numpy as jnp
from jax import lax
from jax.experimental import pallas as pl
from jax.experimental.pallas import tpu as pltpu
from jax.sharding import PartitionSpec as P

retain = 0.9
epsilon = 1e-06
HIGH = lax.Precision.HIGHEST
MESH = pl.DeviceIdType.MESH
NX, NY, NZ, RANK = 4, 8, 8, 256
F32 = jnp.float32


def dot(a, b, ca=1, cb=0):
    return lax.dot_general(
        a, b, (((ca,), (cb,)), ((), ())), precision=HIGH, preferred_element_type=F32
    )


def halves(v):
    high = v.astype(jnp.bfloat16)
    return high, (v - high.astype(F32)).astype(jnp.bfloat16)


def dot_halves(a, b, ca=1, cb=0):
    dims = (((ca,), (cb,)), ((), ()))

    def one(u, v):
        return lax.dot_general(u, v, dims, preferred_element_type=F32)

    return one(a[0], b[0]) + (one(a[0], b[1]) + one(a[1], b[0]))


def invert_half(a, hook=None):
    lanes = lax.broadcasted_iota(jnp.int32, (8, 128), 1)
    subs = lax.broadcasted_iota(jnp.int32, (8, 128), 0)
    groups = [a[8 * g : 8 * g + 8] for g in range(16)]
    done = []
    for k in range(16):
        base = 8 * k
        inside = (lanes >= base) & (lanes < base + 8)
        panel = groups[0]
        cols = [jnp.broadcast_to(panel[:, base + j : base + j + 1], (8, 128)) for j in range(8)]
        held = jnp.where(inside, (lanes == subs + base).astype(F32), panel)
        pivots = cols[0]
        inverse, heads = [], []
        for j in range(8):
            r = 1.0 / cols[j][j : j + 1]
            inverse.append(r)
            mult = jnp.where(subs > j, cols[j] * r, 0.0)
            heads.append([c[j : j + 1] for c in cols])
            for jj in range(j + 1, 8):
                cols[jj] = cols[jj] - mult * heads[j][jj]
            held = held - mult * held[j : j + 1]
            if j:
                pivots = jnp.where(subs == j, cols[j], pivots)
        done.append(jnp.where(lanes <= subs + base, held * lax.rsqrt(pivots), 0.0))
        rest = []
        for g in groups[1:]:
            c = [jnp.broadcast_to(g[:, base + j : base + j + 1], (8, 128)) for j in range(8)]
            out = jnp.where(inside, 0.0, g)
            for j in range(8):
                m = c[j] * inverse[j]
                for jj in range(j + 1, 8):
                    c[jj] = c[jj] - m * heads[j][jj]
                out = out - m * held[j : j + 1]
            rest.append(out)
        groups = rest
        if hook is not None:
            hook(k)
    return jnp.concatenate(done, axis=0)


def place():
    f = lax.axis_index("fsdp")
    return f // 16, lax.rem(f // 2, 8), lax.rem(f, 2), lax.axis_index("tp")


NEAR_FIRST = (1, 7, 2, 6, 3, 5, 4)
FAR_FIRST = (4, 3, 5, 2, 6, 1, 7)


def kernel(
    mom_up, grad_up, basis_up, mom_down, grad_down, basis_down,
    upd_up, new_up, nb_up, upd_down, new_down, nb_down,
    q, wfull, wpart, wcore, wsum, wu_x, wu_s, wu_y, wd_y, wd_s, wd_x,
    m_up, m_down, blend_up, blend_down, r_up, o_upd_up, o_new_up, o_upd_down, o_new_down,
    part_up, part_up_in, pfull_up, part_down, part_down_in, pfull_down,
    gram, gram_in, gsum, g_x, g_y, g_all, xinv, ssum, ssum_in, whole,
    g_up, g_down, bu_hi, bu_lo, pd_hi, pd_lo, tu_hi, tu_lo, td_hi, td_lo,
    send, recv, local,
):
    x, y, c, z = place()
    count = [0]

    def at(xx, yy, cc, zz):
        return (xx * 16 + yy * 2 + cc, zz)

    def along_y(d):
        return at(x, lax.rem(y + d, NY), c, z)

    def along_x(d):
        return at(lax.rem(x + d, NX), y, c, z)

    def along_z(d):
        return at(x, y, c, lax.rem(z + d, NZ))

    sibling = at(x, y, 1 - c, z)

    barrier = pltpu.get_barrier_semaphore()
    peers = (
        [along_y(d) for d in range(1, NY)]
        + [along_x(d) for d in range(1, NX)]
        + [along_z(d) for d in range(1, NZ)]
        + [sibling]
    )
    for peer in peers:
        pl.semaphore_signal(barrier, inc=1, device_id=peer, device_id_type=MESH)
    loads = [
        pltpu.make_async_copy(src, dst, local.at[i])
        for i, (src, dst) in enumerate(
            ((mom_down, m_down), (grad_down, g_down), (mom_up, m_up), (grad_up, g_up))
        )
    ]
    for load in loads:
        load.start()

    sent = [0] * PHASES
    phase = [0]

    def group(rows):
        n = count[0]
        count[0] += 1

        def arrive():
            pltpu.make_async_remote_copy(
                whole.at[0:rows], whole.at[0:rows], send.at[0], recv.at[n],
                device_id=sibling, device_id_type=MESH,
            ).wait_recv()

        arrive.number = n
        return arrive

    def transfer(src, dst, device, to):
        pltpu.make_async_remote_copy(
            src, dst, send.at[phase[0]], recv.at[to.number], device_id=device, device_id_type=MESH
        ).start()
        sent[phase[0]] += math.prod(src.shape) // RANK

    def drain(n):
        pltpu.make_async_remote_copy(
            whole.at[0 : sent[n]], whole.at[0 : sent[n]], send.at[n], recv.at[0],
            device_id=sibling, device_id_type=MESH,
        ).wait_send()

    def back(v, d, n):
        return lax.rem(v + n - d, n)

    down_x = group(24)
    down_y = group(224)
    up_y = {d: group(24) for d in NEAR_FIRST}
    up_x = {d: group(192) for d in range(1, NX)}
    cores = [group(192) for _ in range(NX)] + [group(256)]

    class Gather:
        def __init__(self, buf):
            self.buf = buf
            for d in (2, 1, 3):
                piece = buf.at[x, y, c, 24:32]
                transfer(piece, piece, along_x(d), down_x)
            for d in NEAR_FIRST:
                piece = buf.at[x, y, c, 0:24]
                transfer(piece, piece, along_y(d), up_y[d])
            self.forward(y)

        def forward(self, yy):
            for d in (2, 1, 3):
                piece = self.buf.at[x, yy, c, 0:24]
                transfer(piece, piece, along_x(d), up_x[d])

        def turn(self):
            down_x()
            for d in FAR_FIRST:
                piece = self.buf.at[:, y, c, 24:32]
                transfer(piece, piece, along_y(d), down_y)

        def relay(self, *steps):
            for d in steps:
                up_y[d]()
                self.forward(back(y, d, NY))

        def own(self):
            self.seen = [0]
            self.across(0)

        def across(self, d):
            block = self.buf.at[back(x, d, NX), :, c, 0:24]
            transfer(block, block, sibling, cores[d])

        def column(self, d):
            up_x[d]()
            self.seen.append(d)
            self.across(d)

        def down(self):
            down_y()
            block = self.buf.at[:, :, c, 24:32]
            transfer(block, block, sibling, cores[NX])

        def up(self, use):
            before = 0
            for d in (1, 3, 2):
                if d not in self.seen:
                    self.column(d)
                cores[before]()
                use(back(x, before, NX))
                before = d
            cores[before]()
            use(back(x, before, NX))

    q[x, y, c, 0:24, :] = basis_up[0]
    q[x, y, c, 24:32, :] = jnp.zeros((8, RANK), F32)
    for i in range(6):
        q[x, y, c, 24 + i : 25 + i, :] = basis_down[i]
    pl.semaphore_wait(barrier, len(peers))
    first = Gather(q)

    column = lax.broadcasted_iota(jnp.int32, (384, 512), 0)
    slot = lax.broadcasted_iota(jnp.int32, (384, 512), 1)
    pick = ((column == (slot // 8) * 6 + lax.rem(slot, 8)) & (lax.rem(slot, 8) < 6)).astype(F32)
    for load in loads:
        load.wait()
    blend_down[...] = m_down[...] + g_down[...].astype(F32)
    blend_up[...] = m_up[...] + g_up[...].astype(F32)
    for g in range(NX):
        bu_hi[g], bu_lo[g] = halves(blend_up[:, 384 * g : 384 * g + 384])
    padded = dot(blend_down[...], pick)
    pd_hi[...], pd_lo[...] = halves(padded)
    first.turn()
    first.relay(*NEAR_FIRST)
    first.own()
    first.down()
    cores[NX]()
    phase[0] = 1

    p_part = dot_halves(
        (pd_hi[...], pd_lo[...]), halves(q[:, :, :, 24:32, :].reshape(512, RANK))
    )
    part_down[...] = p_part.reshape(NZ, 24, RANK)

    def reduce_z(part, part_in, to):
        for d in FAR_FIRST:
            transfer(part.at[lax.rem(z + d, NZ)], part_in.at[d - 1], along_z(d), to)

    def gather_z(part, part_in, full, to):
        total = part[z]
        for d in range(1, NZ):
            total = total + part_in[d - 1]
        full[z] = total
        for d in FAR_FIRST:
            transfer(full.at[z], full.at[z], along_z(d), to)

    down_rs, down_ag, up_rs, up_ag = group(168), group(168), group(56), group(56)
    reduce_z(part_down, part_down_in, down_rs)

    sums_up = []

    def add_up(g):
        piece = halves(q[g, :, :, 0:24, :].reshape(384, RANK))
        sums_up.append(dot_halves((bu_hi[g], bu_lo[g]), piece))

    phase[0] = 0
    first.up(add_up)
    phase[0] = 1
    part_up[0:6] = (sums_up[0] + sums_up[1] + sums_up[2] + sums_up[3]).reshape(6, 8, RANK)
    part_up[6:8] = jnp.zeros((2, 8, RANK), F32)
    reduce_z(part_up, part_up_in, up_rs)
    for g in range(NX):
        tu_hi[g], tu_lo[g] = halves(blend_up[:, 384 * g : 384 * g + 384].T)
    td_hi[...], td_lo[...] = halves(padded.T)
    down_rs()
    gather_z(part_down, part_down_in, pfull_down, down_ag)
    up_rs()
    gather_z(part_up, part_up_in, pfull_up, up_ag)

    down_ag()
    p_down = pfull_down[...].reshape(192, RANK)
    gram[1] = dot(p_down, p_down, 0, 0).reshape(NZ, 32, RANK)
    up_ag()
    p_up = pfull_up[0:6].reshape(48, RANK)
    gram[0] = dot(p_up, p_up, 0, 0).reshape(NZ, 32, RANK)
    gram_core, gram_x, gram_y, gram_z, gram_all = [group(n) for n in (32, 24, 56, 56, 144)]
    transfer(gram.at[1 - c, z], gram_in, sibling, gram_core)
    p_halves = halves(p_up)
    core_up = [group(192) for _ in range(NX)]
    core_down = group(256)
    w_x = [group(72) for _ in range(NY)]
    w_y, wd_y_all, wd_x_all = group(168), group(224), group(24)

    def multiply(e):
        g = lax.rem(x + e, NX)
        wpart[g, :, :, 0:24, :] = dot_halves((tu_hi[g], tu_lo[g]), p_halves).reshape(
            NY, 2, 24, RANK
        )
        phase[0] = 2
        transfer(wpart.at[g, :, 1 - c, 0:24], wcore.at[g, :, 0:24], sibling, core_up[e])
        phase[0] = 1

    def join(e):
        g = lax.rem(x + e, NX)
        core_up[e]()
        wsum[g, :, 0:24] = wpart[g, :, c, 0:24] + wcore[g, :, 0:24]

    def scatter_x(e, d):
        yy = lax.rem(y + d, NY)
        phase[0] = 2
        transfer(wsum.at[lax.rem(x + e, NX), yy, 0:24], wu_x.at[e - 1, d], along_x(e), w_x[d])
        phase[0] = 1

    def scatter_y(d):
        w_x[d]()
        wu_s[d] = wsum[x, lax.rem(y + d, NY), 0:24] + wu_x[0, d] + wu_x[1, d] + wu_x[2, d]
        if d:
            phase[0] = 2
            transfer(wu_s.at[d], wu_y.at[d - 1], along_y(d), w_y)
            phase[0] = 1

    multiply(2)
    gram_core()
    gsum[...] = (gram[c, z] + gram_in[...]).reshape(NX, 8, RANK)
    for d in (2, 1, 3):
        transfer(gsum.at[lax.rem(x + d, NX)], g_x.at[d - 1], along_x(d), gram_x)
    multiply(1)
    multiply(3)
    join(2)
    for d in FAR_FIRST + (0,):
        scatter_x(2, d)
    gram_x()
    g_y[y] = gsum[x] + g_x[0] + g_x[1] + g_x[2]
    for d in FAR_FIRST:
        transfer(g_y.at[y], g_y.at[y], along_y(d), gram_y)
    wpart[:, :, :, 24:32, :] = dot_halves((td_hi[...], td_lo[...]), halves(p_down)).reshape(
        NX, NY, 2, 8, RANK
    )
    phase[0] = 2
    transfer(wpart.at[:, :, 1 - c, 24:32], wcore.at[:, :, 24:32], sibling, core_down)
    join(1)
    join(3)
    for d in FAR_FIRST + (0,):
        scatter_x(1, d)
        scatter_x(3, d)
    multiply(0)
    core_down()
    wsum[:, :, 24:32] = wpart[:, :, c, 24:32] + wcore[:, :, 24:32]
    phase[0] = 2
    for d in FAR_FIRST:
        transfer(wsum.at[:, lax.rem(y + d, NY), 24:32], wd_y.at[d - 1], along_y(d), wd_y_all)
    phase[0] = 1
    join(0)
    gram_y()
    row = g_y[0]
    for i in range(1, NY):
        row = row + g_y[i]
    g_all[z, x] = row
    for d in FAR_FIRST:
        transfer(g_all.at[z, x], g_all.at[z, x], along_z(d), gram_z)
    for d in FAR_FIRST[:3]:
        scatter_y(d)
    gram_z()
    for d in (2, 1, 3):
        for piece in (g_all.at[0:4, x], g_all.at[4:8, x, :, 128:256]):
            transfer(piece, piece, along_x(d), gram_all)
    for d in FAR_FIRST[3:]:
        scatter_y(d)
    wd_y_all()
    owned = wsum[:, y, 24:32]
    for d in range(1, NY):
        owned = owned + wd_y[d - 1]
    wd_s[...] = owned
    phase[0] = 2
    for d in (2, 1, 3):
        transfer(wd_s.at[lax.rem(x + d, NX)], wd_x.at[d - 1], along_x(d), wd_x_all)
    scatter_y(0)
    w_y()
    owned = wu_s[0]
    for d in range(1, NY):
        owned = owned + wu_y[d - 1]
    wfull[x, y, c, 0:24, :] = owned
    wd_x_all()
    wfull[x, y, c, 24:32, :] = wd_s[x] + wd_x[0] + wd_x[1] + wd_x[2]
    phase[0] = 3
    last = Gather(wfull)
    gram_all()

    g11, g12, g22 = (
        g_all[0:4, :, :, 0:128].reshape(128, 128),
        g_all[0:4, :, :, 128:256].reshape(128, 128),
        g_all[4:8, :, :, 128:256].reshape(128, 128),
    )

    def hook(k):
        if k == 1:
            last.relay(1, 7)
            last.turn()
        if k == 5:
            last.relay(2, 6)
        if k == 9:
            last.relay(3, 5)
        if k == 12:
            last.relay(4)
            last.own()

    x11 = invert_half(g11, hook)
    xinv[c, 0:128, 0:128] = x11
    xinv[c, 0:128, 128:256] = jnp.zeros((128, 128), F32)
    u = dot(x11, g12)
    low = g22 - dot(u, u, 0, 0)
    corner = dot(u, x11, 0, 0)

    late = []

    def hook(k):
        if k == 6:
            last.down()
        if k == 9:
            last.column(1)
        if k == 11:
            cores[NX]()
            late.append(halves(dot(pick, wfull[:, :, :, 24:32, :].reshape(512, RANK))))
        if k == 12:
            last.column(3)

    x22 = invert_half(low, hook)
    xinv[c, 128:256, 128:256] = x22
    xinv[c, 128:256, 0:128] = -dot(x22, corner)
    x_wait = group(256)
    phase[0] = 1
    transfer(xinv.at[c], xinv.at[c], sibling, x_wait)
    phase[0] = 3
    x_wait()
    x_up, x_down = halves(xinv[0]), halves(xinv[1])

    right_down = dot_halves(late[0], x_down, 1, 1)
    squares = []

    def turn(g):
        right = dot_halves(halves(wfull[g, :, :, 0:24, :].reshape(384, RANK)), x_up, 1, 1)
        r_up[g] = right
        squares.append(jnp.sum(right * right, axis=0, keepdims=True))

    last.up(turn)
    ssum[...] = jnp.zeros((8, RANK), F32)
    ssum[0:1, :] = squares[0] + squares[1] + squares[2] + squares[3]
    ssum[1:2, :] = jnp.sum(right_down * right_down, axis=0, keepdims=True)
    s_wait = group(56)
    phase[0] = 4
    for d in FAR_FIRST:
        transfer(ssum, ssum_in.at[d - 1], along_z(d), s_wait)
    o_up = dot_halves(halves(p_up), x_up, 1, 1)
    o_down = dot_halves(halves(p_down), x_down, 1, 1)
    ou_halves, od_halves = halves(o_up), halves(o_down)
    rd_halves = halves(right_down)
    writes = []

    def write(src, dst):
        copy = pltpu.make_async_copy(src, dst, local.at[4 + len(writes)])
        copy.start()
        writes.append(copy)

    o_new_down[...] = blend_down[...] - (1.0 - retain) * dot_halves(od_halves, rd_halves, 1, 1)
    write(o_new_down, new_down)
    ru_halves = [halves(r_up[g]) for g in range(NX)]
    for g in range(NX):
        cols = slice(384 * g, 384 * g + 384)
        o_new_up[:, cols] = blend_up[:, cols] - (1.0 - retain) * dot_halves(
            ou_halves, ru_halves[g], 1, 1
        )
    write(o_new_up, new_up)
    nb = dot_halves(halves(wfull[x, y, c, 24:32, :]), x_down, 1, 1)
    for n in range(4):
        drain(n)
    s_wait()
    sums = ssum[...]
    for d in range(1, NZ):
        sums = sums + ssum_in[d - 1]
    scale = lax.rsqrt(sums + epsilon)
    s_up, s_down = scale[0:1], scale[1:2]
    ou_halves = halves(math.sqrt(3072 / 12288) * o_up * s_up)
    for g in range(NX):
        o_upd_up[:, 384 * g : 384 * g + 384] = dot_halves(ou_halves, ru_halves[g], 1, 1)
    write(o_upd_up, upd_up)
    od_halves = halves(math.sqrt(12288 / 3072) * o_down * s_down)
    o_upd_down[...] = dot_halves(od_halves, rd_halves, 1, 1)
    write(o_upd_down, upd_down)
    nb_up[0] = r_up[x, pl.ds(pl.multiple_of(48 * y + 24 * c, 8), 24), :] * s_up
    nb = nb * s_down
    for i in range(6):
        nb_down[i] = nb[i : i + 1]
    drain(4)
    for copy in writes:
        copy.wait()


PIECES = (NX, NY, 2, 32, RANK)
SCRATCH = (
    [PIECES, PIECES, PIECES, (NX, NY, 32, RANK), (NX, NY, 32, RANK)]
    + [(NX - 1, NY, 24, RANK), (NY, 24, RANK), (NY - 1, 24, RANK)]
    + [(NY - 1, NX, 8, RANK), (NX, 8, RANK), (NX - 1, 8, RANK)]
    + [(48, 1536), (192, 384), (48, 1536), (192, 384), (NX, 384, RANK)]
    + [(48, 1536), (48, 1536), (192, 384), (192, 384)]
    + [(NZ, 8, RANK), (NZ - 1, 8, RANK), (NZ, 8, RANK)]
    + [(NZ, 24, RANK), (NZ - 1, 24, RANK), (NZ, 24, RANK)]
    + [(2, NZ, 32, RANK), (32, RANK), (NX, 8, RANK), (NX - 1, 8, RANK), (NY, 8, RANK)]
    + [(NZ, NX, 8, RANK)]
    + [(2, RANK, RANK), (8, RANK), (NZ - 1, 8, RANK), (2048, RANK)]
)
HALF_SCRATCH = (
    [(48, 1536), (192, 384)]
    + [(NX, 48, 384)] * 2
    + [(192, 512)] * 2
    + [(NX, 384, 48)] * 2
    + [(512, 192)] * 2
)
PHASES, GROUPS = 5, 56


def finish(*refs):
    sources, results, held, sems = refs[0:6], refs[6:12], refs[12:18], refs[18]
    reads = [pltpu.make_async_copy(a, b, sems.at[0, i]) for i, (a, b) in enumerate(zip(sources, held))]
    writes = [pltpu.make_async_copy(a, b, sems.at[1, i]) for i, (a, b) in enumerate(zip(held, results))]
    for copy in reads:
        copy.start()
    for read, write in zip(reads, writes):
        read.wait()
        write.start()
    for copy in writes:
        copy.wait()


def body(mom_up, grad_up, basis_up, mom_down, grad_down, basis_down):
    vmem = pl.BlockSpec(memory_space=pltpu.VMEM)
    anywhere = pl.BlockSpec(memory_space=pl.ANY)
    shapes = [(48, 1536), (48, 1536), (1, 24, RANK), (192, 384), (192, 384), (6, 1, RANK)]
    out_shape = [jax.ShapeDtypeStruct(s, F32) for s in shapes]
    results = pl.pallas_call(
        kernel,
        out_shape=out_shape,
        in_specs=[anywhere, anywhere, vmem] * 2,
        out_specs=[anywhere, anywhere, vmem] * 2,
        scratch_shapes=[pltpu.VMEM(s, F32) for s in SCRATCH]
        + [pltpu.VMEM(s, jnp.bfloat16) for s in HALF_SCRATCH]
        + [pltpu.SemaphoreType.DMA((n,)) for n in (PHASES, GROUPS)]
        + [pltpu.SemaphoreType.DMA((8,))],
        compiler_params=pltpu.CompilerParams(
            collective_id=0, has_side_effects=True, vmem_limit_bytes=60 << 20
        ),
    )(mom_up, grad_up, basis_up, mom_down, grad_down, jnp.swapaxes(basis_down, 0, 1))
    results = pl.pallas_call(
        finish,
        out_shape=out_shape,
        in_specs=[anywhere] * 6,
        out_specs=[anywhere] * 6,
        scratch_shapes=[pltpu.VMEM(s, F32) for s in shapes] + [pltpu.SemaphoreType.DMA((2, 6))],
    )(*results)
    return (*results[:5], jnp.swapaxes(results[5], 0, 1))


def solution(mesh):
    specs = (P("fsdp", "tp"), P("fsdp", "tp"), P("tp", "fsdp", None)) * 2
    return jax.shard_map(
        body,
        mesh=mesh,
        in_specs=specs,
        out_specs=specs,
        check_vma=False,
    )
```

```python
import math

import jax
import jax.numpy as jnp
from jax import lax
from jax.experimental import pallas as pl
from jax.experimental.pallas import tpu as pltpu
from jax.sharding import PartitionSpec as P

retain = 0.9
epsilon = 1e-06
HIGH = lax.Precision.HIGHEST
MESH = pl.DeviceIdType.MESH
NX, NY, NZ, RANK = 4, 8, 8, 256
F32 = jnp.float32


def dot(a, b, ca=1, cb=0):
    return lax.dot_general(
        a, b, (((ca,), (cb,)), ((), ())), precision=HIGH, preferred_element_type=F32
    )


def halves(v):
    high = v.astype(jnp.bfloat16)
    return high, (v - high.astype(F32)).astype(jnp.bfloat16)


def dot_halves(a, b, ca=1, cb=0):
    dims = (((ca,), (cb,)), ((), ()))

    def one(u, v):
        return lax.dot_general(u, v, dims, preferred_element_type=F32)

    return one(a[0], b[0]) + (one(a[0], b[1]) + one(a[1], b[0]))


def invert_half(a, hook=None):
    lanes = lax.broadcasted_iota(jnp.int32, (8, 128), 1)
    subs = lax.broadcasted_iota(jnp.int32, (8, 128), 0)
    groups = [a[8 * g : 8 * g + 8] for g in range(16)]
    done = []
    for k in range(16):
        base = 8 * k
        inside = (lanes >= base) & (lanes < base + 8)
        panel = groups[0]
        cols = [jnp.broadcast_to(panel[:, base + j : base + j + 1], (8, 128)) for j in range(8)]
        held = jnp.where(inside, (lanes == subs + base).astype(F32), panel)
        pivots = cols[0]
        inverse, heads = [], []
        for j in range(8):
            r = 1.0 / cols[j][j : j + 1]
            inverse.append(r)
            mult = jnp.where(subs > j, cols[j] * r, 0.0)
            heads.append([c[j : j + 1] for c in cols])
            for jj in range(j + 1, 8):
                cols[jj] = cols[jj] - mult * heads[j][jj]
            held = held - mult * held[j : j + 1]
            if j:
                pivots = jnp.where(subs == j, cols[j], pivots)
        done.append(jnp.where(lanes <= subs + base, held * lax.rsqrt(pivots), 0.0))
        rest = []
        for g in groups[1:]:
            c = [jnp.broadcast_to(g[:, base + j : base + j + 1], (8, 128)) for j in range(8)]
            out = jnp.where(inside, 0.0, g)
            for j in range(8):
                m = c[j] * inverse[j]
                for jj in range(j + 1, 8):
                    c[jj] = c[jj] - m * heads[j][jj]
                out = out - m * held[j : j + 1]
            rest.append(out)
        groups = rest
        if hook is not None:
            hook(k)
    return jnp.concatenate(done, axis=0)


def place():
    f = lax.axis_index("fsdp")
    return f // 16, lax.rem(f // 2, 8), lax.rem(f, 2), lax.axis_index("tp")


NEAR_FIRST = (1, 7, 2, 6, 3, 5, 4)
FAR_FIRST = (4, 3, 5, 2, 6, 1, 7)


def kernel(
    mom_up, grad_up, basis_up, mom_down, grad_down, basis_down,
    upd_up, new_up, nb_up, upd_down, new_down, nb_down,
    q, wfull, wpart, wcore, wsum, wu_x, wu_s, wu_y, wd_y, wd_s, wd_x,
    m_up, m_down, blend_up, blend_down, r_up, o_upd_up, o_new_up, o_upd_down, o_new_down,
    part_up, part_up_in, pfull_up, part_down, part_down_in, pfull_down,
    gram, gram_in, gsum, g_x, g_y, g_all, xinv, ssum, ssum_in, whole,
    g_up, g_down, bu_hi, bu_lo, pd_hi, pd_lo, tu_hi, tu_lo, td_hi, td_lo,
    send, recv, local,
):
    x, y, c, z = place()
    count = [0]

    def at(xx, yy, cc, zz):
        return (xx * 16 + yy * 2 + cc, zz)

    def along_y(d):
        return at(x, lax.rem(y + d, NY), c, z)

    def along_x(d):
        return at(lax.rem(x + d, NX), y, c, z)

    def along_z(d):
        return at(x, y, c, lax.rem(z + d, NZ))

    sibling = at(x, y, 1 - c, z)

    barrier = pltpu.get_barrier_semaphore()
    peers = (
        [along_y(d) for d in range(1, NY)]
        + [along_x(d) for d in range(1, NX)]
        + [along_z(d) for d in range(1, NZ)]
        + [sibling]
    )
    for peer in peers:
        pl.semaphore_signal(barrier, inc=1, device_id=peer, device_id_type=MESH)
    loads = [
        pltpu.make_async_copy(src, dst, local.at[i])
        for i, (src, dst) in enumerate(
            ((mom_down, m_down), (grad_down, g_down), (mom_up, m_up), (grad_up, g_up))
        )
    ]
    for load in loads:
        load.start()

    sent = [0] * PHASES
    phase = [0]

    def group(rows):
        n = count[0]
        count[0] += 1

        def arrive(part=1):
            pltpu.make_async_remote_copy(
                whole.at[0 : 2 * rows // part], whole.at[0 : 2 * rows // part], send.at[0], recv.at[n],
                device_id=sibling, device_id_type=MESH,
            ).wait_recv()

        arrive.number = n
        return arrive

    def transfer(src, dst, device, to):
        pltpu.make_async_remote_copy(
            src, dst, send.at[phase[0]], recv.at[to.number], device_id=device, device_id_type=MESH
        ).start()
        sent[phase[0]] += math.prod(src.shape) // 128

    def drain(n):
        pltpu.make_async_remote_copy(
            whole.at[0 : sent[n]], whole.at[0 : sent[n]], send.at[n], recv.at[0],
            device_id=sibling, device_id_type=MESH,
        ).wait_send()

    def back(v, d, n):
        return lax.rem(v + n - d, n)

    down_x = group(24)
    down_y = group(224)
    up_y = [{d: group(24) for d in NEAR_FIRST} for _ in range(2)]
    up_x = [{d: group(192) for d in range(1, NX)} for _ in range(2)]
    cores = [[group(192) for _ in range(NX)] for _ in range(2)]
    core_rest = group(256)

    class Up:
        def __init__(self, buf, lanes, half, part):
            self.buf, self.lanes, self.part = buf, lanes, part
            self.y, self.x, self.cores, self.seen = up_y[half], up_x[half], cores[half], []
            for d in NEAR_FIRST:
                piece = buf.at[x, y, c, 0:24, lanes]
                transfer(piece, piece, along_y(d), self.y[d])
            self.forward(y)

        def forward(self, yy):
            for d in (2, 1, 3):
                piece = self.buf.at[x, yy, c, 0:24, self.lanes]
                transfer(piece, piece, along_x(d), self.x[d])

        def relay(self, *steps):
            for d in steps:
                self.y[d](self.part)
                self.forward(back(y, d, NY))

        def column(self, *steps):
            for d in steps:
                if d in self.seen:
                    continue
                if d:
                    self.x[d](self.part)
                self.seen.append(d)
                block = self.buf.at[back(x, d, NX), :, c, 0:24, self.lanes]
                transfer(block, block, sibling, self.cores[d])

        def arrive(self, d):
            self.cores[d](self.part)

    class Down:
        def __init__(self, buf):
            self.buf = buf
            for d in (2, 1, 3):
                piece = buf.at[x, y, c, 24:32]
                transfer(piece, piece, along_x(d), down_x)

        def turn(self):
            down_x()
            for d in FAR_FIRST:
                piece = self.buf.at[:, y, c, 24:32]
                transfer(piece, piece, along_y(d), down_y)

        def across(self):
            down_y()
            block = self.buf.at[:, :, c, 24:32]
            transfer(block, block, sibling, core_rest)

    def collect(parts, use):
        before = 0
        for d in (1, 3, 2):
            for part in parts:
                part.column(d)
            for part in parts:
                part.arrive(before)
            use(back(x, before, NX))
            before = d
        for part in parts:
            part.arrive(before)
        use(back(x, before, NX))

    q[x, y, c, 0:24, :] = basis_up[0]
    q[x, y, c, 24:32, :] = jnp.zeros((8, RANK), F32)
    for i in range(6):
        q[x, y, c, 24 + i : 25 + i, :] = basis_down[i]
    pl.semaphore_wait(barrier, len(peers))
    first_down = Down(q)
    first_up = Up(q, slice(0, RANK), 0, 1)

    column = lax.broadcasted_iota(jnp.int32, (384, 512), 0)
    slot = lax.broadcasted_iota(jnp.int32, (384, 512), 1)
    pick = ((column == (slot // 8) * 6 + lax.rem(slot, 8)) & (lax.rem(slot, 8) < 6)).astype(F32)
    for load in loads:
        load.wait()
    blend_down[...] = m_down[...] + g_down[...].astype(F32)
    blend_up[...] = m_up[...] + g_up[...].astype(F32)
    for g in range(NX):
        bu_hi[g], bu_lo[g] = halves(blend_up[:, 384 * g : 384 * g + 384])
    padded = dot(blend_down[...], pick)
    pd_hi[...], pd_lo[...] = halves(padded)
    first_down.turn()
    first_up.relay(*NEAR_FIRST)
    first_up.column(0)
    first_down.across()
    core_rest()
    phase[0] = 1

    p_part = dot_halves(
        (pd_hi[...], pd_lo[...]), halves(q[:, :, :, 24:32, :].reshape(512, RANK))
    )
    part_down[...] = p_part.reshape(NZ, 24, RANK)

    def reduce_z(part, part_in, to):
        for d in FAR_FIRST:
            transfer(part.at[lax.rem(z + d, NZ)], part_in.at[d - 1], along_z(d), to)

    def gather_z(part, part_in, full, to):
        total = part[z]
        for d in range(1, NZ):
            total = total + part_in[d - 1]
        full[z] = total
        for d in FAR_FIRST:
            transfer(full.at[z], full.at[z], along_z(d), to)

    down_rs, down_ag, up_rs, up_ag = group(168), group(168), group(56), group(56)
    reduce_z(part_down, part_down_in, down_rs)

    sums_up = []

    def add_up(g):
        piece = halves(q[g, :, :, 0:24, :].reshape(384, RANK))
        sums_up.append(dot_halves((bu_hi[g], bu_lo[g]), piece))

    phase[0] = 0
    collect([first_up], add_up)
    phase[0] = 1
    part_up[0:6] = (sums_up[0] + sums_up[1] + sums_up[2] + sums_up[3]).reshape(6, 8, RANK)
    part_up[6:8] = jnp.zeros((2, 8, RANK), F32)
    reduce_z(part_up, part_up_in, up_rs)
    for g in range(NX):
        tu_hi[g], tu_lo[g] = halves(blend_up[:, 384 * g : 384 * g + 384].T)
    td_hi[...], td_lo[...] = halves(padded.T)
    down_rs()
    gather_z(part_down, part_down_in, pfull_down, down_ag)
    up_rs()
    gather_z(part_up, part_up_in, pfull_up, up_ag)

    down_ag()
    p_down = pfull_down[...].reshape(192, RANK)
    gram[1] = dot(p_down, p_down, 0, 0).reshape(NZ, 32, RANK)
    up_ag()
    p_up = pfull_up[0:6].reshape(48, RANK)
    gram[0] = dot(p_up, p_up, 0, 0).reshape(NZ, 32, RANK)
    gram_core, gram_x, gram_y, gram_z, gram_all = [group(n) for n in (32, 24, 56, 56, 144)]
    transfer(gram.at[1 - c, z], gram_in, sibling, gram_core)
    p_halves = halves(p_up)
    core_up = [group(192) for _ in range(NX)]
    core_down = group(256)
    w_x = [[group(36) for _ in range(NY)] for _ in range(2)]
    w_y = [group(84), group(84)]
    wd_y_all, wd_x_all = group(224), group(24)
    sides = [slice(0, 128), slice(128, 256)]

    def multiply(e):
        g = lax.rem(x + e, NX)
        wpart[g, :, :, 0:24, :] = dot_halves((tu_hi[g], tu_lo[g]), p_halves).reshape(
            NY, 2, 24, RANK
        )
        phase[0] = 2
        transfer(wpart.at[g, :, 1 - c, 0:24], wcore.at[g, :, 0:24], sibling, core_up[e])
        phase[0] = 1

    def join(e):
        g = lax.rem(x + e, NX)
        core_up[e]()
        wsum[g, :, 0:24] = wpart[g, :, c, 0:24] + wcore[g, :, 0:24]

    def scatter_x(e, d, h):
        phase[0] = 2
        transfer(
            wsum.at[lax.rem(x + e, NX), lax.rem(y + d, NY), 0:24, sides[h]],
            wu_x.at[e - 1, d, :, sides[h]], along_x(e), w_x[h][d],
        )
        phase[0] = 1

    def scatter_y(h, *steps):
        lanes = sides[h]
        for d in steps:
            w_x[h][d]()
            wu_s[d, :, lanes] = (
                wsum[x, lax.rem(y + d, NY), 0:24, lanes]
                + wu_x[0, d, :, lanes] + wu_x[1, d, :, lanes] + wu_x[2, d, :, lanes]
            )
            if d:
                phase[0] = 2
                transfer(wu_s.at[d, :, lanes], wu_y.at[d - 1, :, lanes], along_y(d), w_y[h])
                phase[0] = 1

    def own_piece(h):
        lanes = sides[h]
        w_y[h]()
        owned = wu_s[0, :, lanes]
        for d in range(1, NY):
            owned = owned + wu_y[d - 1, :, lanes]
        wfull[x, y, c, 0:24, lanes] = owned
        phase[0] = 3
        gathers.append(Up(wfull, lanes, h, 2))
        phase[0] = 1

    gathers = []
    multiply(2)
    gram_core()
    gsum[...] = (gram[c, z] + gram_in[...]).reshape(NX, 8, RANK)
    for d in (2, 1, 3):
        transfer(gsum.at[lax.rem(x + d, NX)], g_x.at[d - 1], along_x(d), gram_x)
    multiply(1)
    multiply(3)
    join(2)
    for d in FAR_FIRST + (0,):
        scatter_x(2, d, 0)
    multiply(0)
    gram_x()
    g_y[y] = gsum[x] + g_x[0] + g_x[1] + g_x[2]
    for d in FAR_FIRST:
        transfer(g_y.at[y], g_y.at[y], along_y(d), gram_y)
    wpart[:, :, :, 24:32, :] = dot_halves((td_hi[...], td_lo[...]), halves(p_down)).reshape(
        NX, NY, 2, 8, RANK
    )
    phase[0] = 2
    transfer(wpart.at[:, :, 1 - c, 24:32], wcore.at[:, :, 24:32], sibling, core_down)
    join(1)
    join(3)
    for d in FAR_FIRST + (0,):
        scatter_x(1, d, 0)
        scatter_x(3, d, 0)
    for d in FAR_FIRST + (0,):
        scatter_x(2, d, 1)
        scatter_x(1, d, 1)
        scatter_x(3, d, 1)
    core_down()
    wsum[:, :, 24:32] = wpart[:, :, c, 24:32] + wcore[:, :, 24:32]
    phase[0] = 2
    for d in FAR_FIRST:
        transfer(wsum.at[:, lax.rem(y + d, NY), 24:32], wd_y.at[d - 1], along_y(d), wd_y_all)
    phase[0] = 1
    join(0)
    gram_y()
    row = g_y[0]
    for i in range(1, NY):
        row = row + g_y[i]
    g_all[z, x] = row
    for d in FAR_FIRST:
        transfer(g_all.at[z, x], g_all.at[z, x], along_z(d), gram_z)
    scatter_y(0, *FAR_FIRST, 0)
    scatter_y(1, *FAR_FIRST[:4])
    gram_z()
    for d in (2, 1, 3):
        for piece in (g_all.at[0:4, x], g_all.at[4:8, x, :, 128:256]):
            transfer(piece, piece, along_x(d), gram_all)
    wd_y_all()
    owned = wsum[:, y, 24:32]
    for d in range(1, NY):
        owned = owned + wd_y[d - 1]
    wd_s[...] = owned
    phase[0] = 2
    for d in (2, 1, 3):
        transfer(wd_s.at[lax.rem(x + d, NX)], wd_x.at[d - 1], along_x(d), wd_x_all)
    phase[0] = 1
    scatter_y(1, *FAR_FIRST[4:], 0)
    own_piece(0)
    wd_x_all()
    wfull[x, y, c, 24:32, :] = wd_s[x] + wd_x[0] + wd_x[1] + wd_x[2]
    phase[0] = 3
    rest = Down(wfull)
    gram_all()

    g11, g12, g22 = (
        g_all[0:4, :, :, 0:128].reshape(128, 128),
        g_all[0:4, :, :, 128:256].reshape(128, 128),
        g_all[4:8, :, :, 128:256].reshape(128, 128),
    )

    def hook(k):
        if k == 0:
            own_piece(1)
            phase[0] = 3
        if k == 1:
            gathers[0].relay(1, 7)
        if k == 3:
            gathers[0].relay(2, 6)
        if k == 5:
            rest.turn()
        if k == 7:
            gathers[1].relay(1, 7)
        if k == 8:
            gathers[0].relay(3, 5, 4)
            gathers[0].column(0)
        if k == 11:
            gathers[1].relay(2, 6)
        if k == 15:
            gathers[1].relay(3, 5)

    x11 = invert_half(g11, hook)
    xinv[c, 0:128, 0:128] = x11
    xinv[c, 0:128, 128:256] = jnp.zeros((128, 128), F32)
    u = dot(x11, g12)
    low = g22 - dot(u, u, 0, 0)
    corner = dot(u, x11, 0, 0)

    late = []

    def hook(k):
        if k == 0:
            gathers[1].relay(4)
            gathers[1].column(0)
        if k == 4:
            gathers[0].column(1, 3)
        if k == 7:
            gathers[0].column(2)
        if k == 11:
            gathers[1].column(1, 3)
        if k == 13:
            rest.across()

    x22 = invert_half(low, hook)
    xinv[c, 128:256, 128:256] = x22
    xinv[c, 128:256, 0:128] = -dot(x22, corner)
    x_wait = group(256)
    phase[0] = 1
    transfer(xinv.at[c], xinv.at[c], sibling, x_wait)
    phase[0] = 3
    x_wait()
    x_up, x_down = halves(xinv[0]), halves(xinv[1])

    core_rest()
    late.append(halves(dot(pick, wfull[:, :, :, 24:32, :].reshape(512, RANK))))
    right_down = dot_halves(late[0], x_down, 1, 1)
    squares = []

    def turn(g):
        right = dot_halves(halves(wfull[g, :, :, 0:24, :].reshape(384, RANK)), x_up, 1, 1)
        r_up[g] = right
        squares.append(jnp.sum(right * right, axis=0, keepdims=True))

    collect(gathers, turn)
    ssum[...] = jnp.zeros((8, RANK), F32)
    ssum[0:1, :] = squares[0] + squares[1] + squares[2] + squares[3]
    ssum[1:2, :] = jnp.sum(right_down * right_down, axis=0, keepdims=True)
    s_wait = group(56)
    phase[0] = 4
    for d in FAR_FIRST:
        transfer(ssum, ssum_in.at[d - 1], along_z(d), s_wait)
    o_up = dot_halves(halves(p_up), x_up, 1, 1)
    o_down = dot_halves(halves(p_down), x_down, 1, 1)
    ou_halves, od_halves = halves(o_up), halves(o_down)
    rd_halves = halves(right_down)
    writes = []

    def write(src, dst):
        copy = pltpu.make_async_copy(src, dst, local.at[4 + len(writes)])
        copy.start()
        writes.append(copy)

    o_new_down[...] = blend_down[...] - (1.0 - retain) * dot_halves(od_halves, rd_halves, 1, 1)
    write(o_new_down, new_down)
    ru_halves = [halves(r_up[g]) for g in range(NX)]
    for g in range(NX):
        cols = slice(384 * g, 384 * g + 384)
        o_new_up[:, cols] = blend_up[:, cols] - (1.0 - retain) * dot_halves(
            ou_halves, ru_halves[g], 1, 1
        )
    write(o_new_up, new_up)
    nb = dot_halves(halves(wfull[x, y, c, 24:32, :]), x_down, 1, 1)
    for n in range(4):
        drain(n)
    s_wait()
    sums = ssum[...]
    for d in range(1, NZ):
        sums = sums + ssum_in[d - 1]
    scale = lax.rsqrt(sums + epsilon)
    s_up, s_down = scale[0:1], scale[1:2]
    ou_halves = halves(math.sqrt(3072 / 12288) * o_up * s_up)
    for g in range(NX):
        o_upd_up[:, 384 * g : 384 * g + 384] = dot_halves(ou_halves, ru_halves[g], 1, 1)
    write(o_upd_up, upd_up)
    od_halves = halves(math.sqrt(12288 / 3072) * o_down * s_down)
    o_upd_down[...] = dot_halves(od_halves, rd_halves, 1, 1)
    write(o_upd_down, upd_down)
    nb_up[0] = r_up[x, pl.ds(pl.multiple_of(48 * y + 24 * c, 8), 24), :] * s_up
    nb = nb * s_down
    for i in range(6):
        nb_down[i] = nb[i : i + 1]
    drain(4)
    for copy in writes:
        copy.wait()


PIECES = (NX, NY, 2, 32, RANK)
SCRATCH = (
    [PIECES, PIECES, PIECES, (NX, NY, 32, RANK), (NX, NY, 32, RANK)]
    + [(NX - 1, NY, 24, RANK), (NY, 24, RANK), (NY - 1, 24, RANK)]
    + [(NY - 1, NX, 8, RANK), (NX, 8, RANK), (NX - 1, 8, RANK)]
    + [(48, 1536), (192, 384), (48, 1536), (192, 384), (NX, 384, RANK)]
    + [(48, 1536), (48, 1536), (192, 384), (192, 384)]
    + [(NZ, 8, RANK), (NZ - 1, 8, RANK), (NZ, 8, RANK)]
    + [(NZ, 24, RANK), (NZ - 1, 24, RANK), (NZ, 24, RANK)]
    + [(2, NZ, 32, RANK), (32, RANK), (NX, 8, RANK), (NX - 1, 8, RANK), (NY, 8, RANK)]
    + [(NZ, NX, 8, RANK)]
    + [(2, RANK, RANK), (8, RANK), (NZ - 1, 8, RANK), (4096, 128)]
)
HALF_SCRATCH = (
    [(48, 1536), (192, 384)]
    + [(NX, 48, 384)] * 2
    + [(192, 512)] * 2
    + [(NX, 384, 48)] * 2
    + [(512, 192)] * 2
)
PHASES, GROUPS = 5, 80


def finish(*refs):
    sources, results, held, sems = refs[0:6], refs[6:12], refs[12:18], refs[18]
    reads = [pltpu.make_async_copy(a, b, sems.at[0, i]) for i, (a, b) in enumerate(zip(sources, held))]
    writes = [pltpu.make_async_copy(a, b, sems.at[1, i]) for i, (a, b) in enumerate(zip(held, results))]
    for copy in reads:
        copy.start()
    for read, write in zip(reads, writes):
        read.wait()
        write.start()
    for copy in writes:
        copy.wait()


def body(mom_up, grad_up, basis_up, mom_down, grad_down, basis_down):
    vmem = pl.BlockSpec(memory_space=pltpu.VMEM)
    anywhere = pl.BlockSpec(memory_space=pl.ANY)
    shapes = [(48, 1536), (48, 1536), (1, 24, RANK), (192, 384), (192, 384), (6, 1, RANK)]
    out_shape = [jax.ShapeDtypeStruct(s, F32) for s in shapes]
    results = pl.pallas_call(
        kernel,
        out_shape=out_shape,
        in_specs=[anywhere, anywhere, vmem] * 2,
        out_specs=[anywhere, anywhere, vmem] * 2,
        scratch_shapes=[pltpu.VMEM(s, F32) for s in SCRATCH]
        + [pltpu.VMEM(s, jnp.bfloat16) for s in HALF_SCRATCH]
        + [pltpu.SemaphoreType.DMA((n,)) for n in (PHASES, GROUPS)]
        + [pltpu.SemaphoreType.DMA((8,))],
        compiler_params=pltpu.CompilerParams(
            collective_id=0, has_side_effects=True, vmem_limit_bytes=60 << 20
        ),
    )(mom_up, grad_up, basis_up, mom_down, grad_down, jnp.swapaxes(basis_down, 0, 1))
    results = pl.pallas_call(
        finish,
        out_shape=out_shape,
        in_specs=[anywhere] * 6,
        out_specs=[anywhere] * 6,
        scratch_shapes=[pltpu.VMEM(s, F32) for s in shapes] + [pltpu.SemaphoreType.DMA((2, 6))],
    )(*results)
    return (*results[:5], jnp.swapaxes(results[5], 0, 1))


def solution(mesh):
    specs = (P("fsdp", "tp"), P("fsdp", "tp"), P("tp", "fsdp", None)) * 2
    return jax.shard_map(
        body,
        mesh=mesh,
        in_specs=specs,
        out_specs=specs,
        check_vma=False,
    )
```

```python
import math

import jax
import jax.numpy as jnp
from jax import lax
from jax.experimental import pallas as pl
from jax.experimental.pallas import tpu as pltpu
from jax.sharding import PartitionSpec as P

retain = 0.9
epsilon = 1e-06
HIGH = lax.Precision.HIGHEST
MESH = pl.DeviceIdType.MESH
NX, NY, NZ, RANK = 4, 8, 8, 256
F32 = jnp.float32


def dot(a, b, ca=1, cb=0):
    return lax.dot_general(
        a, b, (((ca,), (cb,)), ((), ())), precision=HIGH, preferred_element_type=F32
    )


def halves(v):
    high = v.astype(jnp.bfloat16)
    return high, (v - high.astype(F32)).astype(jnp.bfloat16)


def dot_halves(a, b, ca=1, cb=0):
    dims = (((ca,), (cb,)), ((), ()))

    def one(u, v):
        return lax.dot_general(u, v, dims, preferred_element_type=F32)

    return one(a[0], b[0]) + (one(a[0], b[1]) + one(a[1], b[0]))


def invert_half(a, hook=None):
    lanes = lax.broadcasted_iota(jnp.int32, (8, 128), 1)
    subs = lax.broadcasted_iota(jnp.int32, (8, 128), 0)
    groups = [a[8 * g : 8 * g + 8] for g in range(16)]
    done = []
    for k in range(16):
        base = 8 * k
        inside = (lanes >= base) & (lanes < base + 8)
        panel = groups[0]
        cols = [jnp.broadcast_to(panel[:, base + j : base + j + 1], (8, 128)) for j in range(8)]
        held = jnp.where(inside, (lanes == subs + base).astype(F32), panel)
        pivots = cols[0]
        inverse, heads = [], []
        for j in range(8):
            r = 1.0 / cols[j][j : j + 1]
            inverse.append(r)
            mult = jnp.where(subs > j, cols[j] * r, 0.0)
            heads.append([c[j : j + 1] for c in cols])
            for jj in range(j + 1, 8):
                cols[jj] = cols[jj] - mult * heads[j][jj]
            held = held - mult * held[j : j + 1]
            if j:
                pivots = jnp.where(subs == j, cols[j], pivots)
        done.append(jnp.where(lanes <= subs + base, held * lax.rsqrt(pivots), 0.0))
        rest = []
        for g in groups[1:]:
            c = [jnp.broadcast_to(g[:, base + j : base + j + 1], (8, 128)) for j in range(8)]
            out = jnp.where(inside, 0.0, g)
            for j in range(8):
                m = c[j] * inverse[j]
                for jj in range(j + 1, 8):
                    c[jj] = c[jj] - m * heads[j][jj]
                out = out - m * held[j : j + 1]
            rest.append(out)
        groups = rest
        if hook is not None:
            hook(k)
    return jnp.concatenate(done, axis=0)


def place():
    f = lax.axis_index("fsdp")
    return f // 16, lax.rem(f // 2, 8), lax.rem(f, 2), lax.axis_index("tp")


NEAR_FIRST = (1, 7, 2, 6, 3, 5, 4)
FAR_FIRST = (4, 3, 5, 2, 6, 1, 7)


def kernel(
    mom_up, grad_up, basis_up, mom_down, grad_down, basis_down,
    upd_up, new_up, nb_up, upd_down, new_down, nb_down,
    q, wfull, wpart, wcore, wsum, wu_x, wu_s, wu_y, wd_y, wd_s, wd_x,
    m_up, m_down, blend_up, blend_down, o_upd_up, o_new_up, o_upd_down, o_new_down,
    part_up, part_up_in, pfull_up, part_down, part_down_in, pfull_down,
    turned_up, turned_down, gram, gram_in, gsum, g_x, g_y, g_all, xinv, ssum, ssum_in, whole,
    g_up, g_down, bu_hi, bu_lo, pd_hi, pd_lo, tu_hi, tu_lo, td_hi, td_lo, wd_half,
    send, recv, local,
):
    x, y, c, z = place()
    count = [0]

    def at(xx, yy, cc, zz):
        return (xx * 16 + yy * 2 + cc, zz)

    def along_y(d):
        return at(x, lax.rem(y + d, NY), c, z)

    def along_x(d):
        return at(lax.rem(x + d, NX), y, c, z)

    def along_z(d):
        return at(x, y, c, lax.rem(z + d, NZ))

    sibling = at(x, y, 1 - c, z)

    barrier = pltpu.get_barrier_semaphore()
    peers = (
        [along_y(d) for d in range(1, NY)]
        + [along_x(d) for d in range(1, NX)]
        + [along_z(d) for d in range(1, NZ)]
        + [at(x, y, 1 - c, lax.rem(z + d, NZ)) for d in range(1, NZ)]
        + [sibling]
    )
    for peer in peers:
        pl.semaphore_signal(barrier, inc=1, device_id=peer, device_id_type=MESH)
    loads = [
        pltpu.make_async_copy(src, dst, local.at[i])
        for i, (src, dst) in enumerate(
            ((mom_down, m_down), (grad_down, g_down), (mom_up, m_up), (grad_up, g_up))
        )
    ]
    for load in loads:
        load.start()

    sent = [0] * PHASES
    phase = [0]

    def group(rows):
        n = count[0]
        count[0] += 1

        def arrive(part=1):
            pltpu.make_async_remote_copy(
                whole.at[0 : 2 * rows // part], whole.at[0 : 2 * rows // part], send.at[0], recv.at[n],
                device_id=sibling, device_id_type=MESH,
            ).wait_recv()

        arrive.number = n
        return arrive

    def transfer(src, dst, device, to):
        pltpu.make_async_remote_copy(
            src, dst, send.at[phase[0]], recv.at[to.number], device_id=device, device_id_type=MESH
        ).start()
        sent[phase[0]] += math.prod(src.shape) // 128

    def drain(n):
        pltpu.make_async_remote_copy(
            whole.at[0 : sent[n]], whole.at[0 : sent[n]], send.at[n], recv.at[0],
            device_id=sibling, device_id_type=MESH,
        ).wait_send()

    def back(v, d, n):
        return lax.rem(v + n - d, n)

    down_x = group(24)
    down_y = group(224)
    up_y = [{d: group(24) for d in NEAR_FIRST} for _ in range(2)]
    up_x = [{d: group(192) for d in range(1, NX)} for _ in range(2)]
    cores = [[group(192) for _ in range(NX)] for _ in range(2)]
    core_rest = group(256)

    class Up:
        def __init__(self, buf, lanes, half, part):
            self.buf, self.lanes, self.part = buf, lanes, part
            self.y, self.x, self.cores, self.seen = up_y[half], up_x[half], cores[half], []
            for d in NEAR_FIRST:
                piece = buf.at[x, y, c, 0:24, lanes]
                transfer(piece, piece, along_y(d), self.y[d])
            self.forward(y)

        def forward(self, yy):
            for d in (2, 1, 3):
                piece = self.buf.at[x, yy, c, 0:24, self.lanes]
                transfer(piece, piece, along_x(d), self.x[d])

        def relay(self, *steps):
            for d in steps:
                self.y[d](self.part)
                self.forward(back(y, d, NY))

        def column(self, *steps):
            for d in steps:
                if d in self.seen:
                    continue
                if d:
                    self.x[d](self.part)
                self.seen.append(d)
                block = self.buf.at[back(x, d, NX), :, c, 0:24, self.lanes]
                transfer(block, block, sibling, self.cores[d])

        def arrive(self, d):
            self.cores[d](self.part)

    class Down:
        def __init__(self, buf):
            self.buf = buf
            for d in (2, 1, 3):
                piece = buf.at[x, y, c, 24:32]
                transfer(piece, piece, along_x(d), down_x)

        def turn(self):
            down_x()
            for d in FAR_FIRST:
                piece = self.buf.at[:, y, c, 24:32]
                transfer(piece, piece, along_y(d), down_y)

        def across(self):
            down_y()
            block = self.buf.at[:, :, c, 24:32]
            transfer(block, block, sibling, core_rest)

    def collect(parts, use):
        before = 0
        for d in (1, 3, 2):
            for part in parts:
                part.column(d)
            for part in parts:
                part.arrive(before)
            use(back(x, before, NX))
            before = d
        for part in parts:
            part.arrive(before)
        use(back(x, before, NX))

    q[x, y, c, 0:24, :] = basis_up[0]
    q[x, y, c, 24:32, :] = jnp.zeros((8, RANK), F32)
    for i in range(6):
        q[x, y, c, 24 + i : 25 + i, :] = basis_down[i]
    pl.semaphore_wait(barrier, len(peers))
    first_down = Down(q)
    first_up = Up(q, slice(0, RANK), 0, 1)

    column = lax.broadcasted_iota(jnp.int32, (384, 512), 0)
    slot = lax.broadcasted_iota(jnp.int32, (384, 512), 1)
    pick = ((column == (slot // 8) * 6 + lax.rem(slot, 8)) & (lax.rem(slot, 8) < 6)).astype(F32)
    for load in loads:
        load.wait()
    blend_down[...] = m_down[...] + g_down[...].astype(F32)
    blend_up[...] = m_up[...] + g_up[...].astype(F32)
    for g in range(NX):
        bu_hi[g], bu_lo[g] = halves(blend_up[:, 384 * g : 384 * g + 384])
    padded = dot(blend_down[...], pick)
    pd_hi[...], pd_lo[...] = halves(padded)
    first_down.turn()
    first_up.relay(*NEAR_FIRST)
    first_up.column(0)
    first_down.across()
    core_rest()
    phase[0] = 1

    p_part = dot_halves(
        (pd_hi[...], pd_lo[...]), halves(q[:, :, :, 24:32, :].reshape(512, RANK))
    )
    part_down[...] = p_part.reshape(NZ, 24, RANK)

    def reduce_z(part, part_in, to):
        for d in FAR_FIRST:
            transfer(part.at[lax.rem(z + d, NZ)], part_in.at[d - 1], along_z(d), to)

    def gather_z(part, part_in, full, to):
        total = part[z]
        for d in range(1, NZ):
            total = total + part_in[d - 1]
        full[z] = total
        for d in FAR_FIRST:
            transfer(full.at[z], full.at[z], along_z(d), to)

    down_rs, down_ag, up_rs, up_ag = group(168), group(168), group(56), group(56)
    reduce_z(part_down, part_down_in, down_rs)

    sums_up = []

    def add_up(g):
        piece = halves(q[g, :, :, 0:24, :].reshape(384, RANK))
        sums_up.append(dot_halves((bu_hi[g], bu_lo[g]), piece))

    phase[0] = 0
    collect([first_up], add_up)
    phase[0] = 1
    part_up[0:6] = (sums_up[0] + sums_up[1] + sums_up[2] + sums_up[3]).reshape(6, 8, RANK)
    part_up[6:8] = jnp.zeros((2, 8, RANK), F32)
    reduce_z(part_up, part_up_in, up_rs)
    for g in range(NX):
        tu_hi[g], tu_lo[g] = halves(blend_up[:, 384 * g : 384 * g + 384].T)
    td_hi[...], td_lo[...] = halves(padded.T)
    down_rs()
    gather_z(part_down, part_down_in, pfull_down, down_ag)
    up_rs()
    gather_z(part_up, part_up_in, pfull_up, up_ag)

    down_ag()
    p_down = pfull_down[...].reshape(192, RANK)
    rows = pl.ds(pl.multiple_of(32 * z, 8), 32)
    turned_down[...] = p_down.T
    gram[1] = dot(turned_down[rows, :], p_down)
    up_ag()
    p_up = pfull_up[0:6].reshape(48, RANK)
    turned_up[...] = p_up.T
    gram[0] = dot(turned_up[rows, :], p_up)
    gram_core, gram_x, gram_y, gram_z, gram_all = [group(n) for n in (32, 24, 56, 56, 144)]
    transfer(gram.at[1 - c], gram_in, sibling, gram_core)
    p_halves = halves(p_up)
    core_up = [group(192) for _ in range(NX)]
    core_down = group(256)
    w_x = [[group(36) for _ in range(NY)] for _ in range(2)]
    w_y = [group(84), group(84)]
    wd_y_all, wd_x_all = group(224), group(24)
    sides = [slice(0, 128), slice(128, 256)]

    def multiply(e):
        g = lax.rem(x + e, NX)
        wpart[g, :, :, 0:24, :] = dot_halves((tu_hi[g], tu_lo[g]), p_halves).reshape(
            NY, 2, 24, RANK
        )
        phase[0] = 2
        transfer(wpart.at[g, :, 1 - c, 0:24], wcore.at[g, :, 0:24], sibling, core_up[e])
        phase[0] = 1

    def join(e):
        g = lax.rem(x + e, NX)
        core_up[e]()
        wsum[g, :, 0:24] = wpart[g, :, c, 0:24] + wcore[g, :, 0:24]

    def scatter_x(e, d, h):
        phase[0] = 2
        transfer(
            wsum.at[lax.rem(x + e, NX), lax.rem(y + d, NY), 0:24, sides[h]],
            wu_x.at[e - 1, d, :, sides[h]], along_x(e), w_x[h][d],
        )
        phase[0] = 1

    def scatter_y(h, *steps):
        lanes = sides[h]
        for d in steps:
            w_x[h][d]()
            wu_s[d, :, lanes] = (
                wsum[x, lax.rem(y + d, NY), 0:24, lanes]
                + wu_x[0, d, :, lanes] + wu_x[1, d, :, lanes] + wu_x[2, d, :, lanes]
            )
            if d:
                phase[0] = 2
                transfer(wu_s.at[d, :, lanes], wu_y.at[d - 1, :, lanes], along_y(d), w_y[h])
                phase[0] = 1

    def own_piece(h):
        lanes = sides[h]
        w_y[h]()
        owned = wu_s[0, :, lanes]
        for d in range(1, NY):
            owned = owned + wu_y[d - 1, :, lanes]
        wfull[x, y, c, 0:24, lanes] = owned
        phase[0] = 3
        gathers.append(Up(wfull, lanes, h, 2))
        phase[0] = 1

    gathers = []
    multiply(2)
    gram_core()
    gsum[...] = (gram[c] + gram_in[...]).reshape(NX, 8, RANK)
    for d in (2, 1, 3):
        transfer(gsum.at[lax.rem(x + d, NX)], g_x.at[d - 1], along_x(d), gram_x)
    multiply(1)
    multiply(3)
    join(2)
    for d in FAR_FIRST + (0,):
        scatter_x(2, d, 0)
    multiply(0)
    gram_x()
    g_y[y] = gsum[x] + g_x[0] + g_x[1] + g_x[2]
    for d in FAR_FIRST:
        transfer(g_y.at[y], g_y.at[y], along_y(d), gram_y)
    wpart[:, :, :, 24:32, :] = dot_halves((td_hi[...], td_lo[...]), halves(p_down)).reshape(
        NX, NY, 2, 8, RANK
    )
    phase[0] = 2
    transfer(wpart.at[:, :, 1 - c, 24:32], wcore.at[:, :, 24:32], sibling, core_down)
    join(1)
    join(3)
    for d in FAR_FIRST + (0,):
        scatter_x(1, d, 0)
        scatter_x(3, d, 0)
    for d in FAR_FIRST + (0,):
        scatter_x(2, d, 1)
        scatter_x(1, d, 1)
        scatter_x(3, d, 1)
    core_down()
    wsum[:, :, 24:32] = wpart[:, :, c, 24:32] + wcore[:, :, 24:32]
    phase[0] = 2
    for d in FAR_FIRST:
        transfer(wsum.at[:, lax.rem(y + d, NY), 24:32], wd_y.at[d - 1], along_y(d), wd_y_all)
    phase[0] = 1
    join(0)
    gram_y()
    row = g_y[0]
    for i in range(1, NY):
        row = row + g_y[i]
    g_all[z, x] = row
    for d in FAR_FIRST:
        transfer(g_all.at[z, x], g_all.at[z, x], along_z(d), gram_z)
    scatter_y(0, *FAR_FIRST, 0)
    scatter_y(1, *FAR_FIRST[:4])
    gram_z()
    for d in (2, 1, 3):
        for piece in (g_all.at[0:4, x], g_all.at[4:8, x, :, 128:256]):
            transfer(piece, piece, along_x(d), gram_all)
    wd_y_all()
    owned = wsum[:, y, 24:32]
    for d in range(1, NY):
        owned = owned + wd_y[d - 1]
    wd_s[...] = owned
    phase[0] = 2
    for d in (2, 1, 3):
        transfer(wd_s.at[lax.rem(x + d, NX)], wd_x.at[d - 1], along_x(d), wd_x_all)
    phase[0] = 1
    scatter_y(1, *FAR_FIRST[4:], 0)
    own_piece(0)
    wd_x_all()
    wfull[x, y, c, 24:32, :] = wd_s[x] + wd_x[0] + wd_x[1] + wd_x[2]
    phase[0] = 3
    rest = Down(wfull)
    gram_all()

    g11, g12, g22 = (
        g_all[0:4, :, :, 0:128].reshape(128, 128),
        g_all[0:4, :, :, 128:256].reshape(128, 128),
        g_all[4:8, :, :, 128:256].reshape(128, 128),
    )

    def hook(k):
        if k == 0:
            own_piece(1)
            phase[0] = 3
        if k == 1:
            gathers[0].relay(1, 7)
        if k == 3:
            gathers[0].relay(2, 6)
        if k == 5:
            rest.turn()
        if k == 7:
            gathers[1].relay(1, 7)
        if k == 8:
            gathers[0].relay(3, 5, 4)
            gathers[0].column(0)
        if k == 11:
            gathers[1].relay(2, 6)
        if k == 15:
            gathers[1].relay(3, 5)

    x11 = invert_half(g11, hook)
    xinv[c, 0:128, 0:128] = x11
    xinv[c, 0:128, 128:256] = jnp.zeros((128, 128), F32)
    u = dot(x11, g12)
    low = g22 - dot(u, u, 0, 0)
    corner = dot(u, x11, 0, 0)

    late = []

    def hook(k):
        if k == 0:
            gathers[1].relay(4)
            gathers[1].column(0)
        if k == 4:
            gathers[0].column(1, 3)
        if k == 7:
            gathers[0].column(2)
        if k == 11:
            gathers[1].column(1, 3)
        if k == 13:
            rest.across()

    x22 = invert_half(low, hook)
    xinv[c, 128:256, 128:256] = x22
    xinv[c, 128:256, 0:128] = -dot(x22, corner)
    x_wait = group(256)
    phase[0] = 1
    transfer(xinv.at[c], xinv.at[c], sibling, x_wait)
    phase[0] = 3
    core_rest()
    select = pick.astype(jnp.bfloat16)
    for i, half in enumerate(halves(wfull[:, :, :, 24:32, :].reshape(512, RANK))):
        rows = lax.dot_general(
            select, half, (((1,), (0,)), ((), ())), preferred_element_type=F32
        )
        wd_half[i] = rows.astype(jnp.bfloat16).reshape(2, 192, RANK)
    x_wait()
    x_up, x_down = halves(xinv[0]), halves(xinv[1])
    right = dot_halves((wd_half[0, c], wd_half[1, c]), x_down, 1, 1)
    sum_down = jnp.sum(right * right, axis=0, keepdims=True)
    collect(gathers, lambda g: None)
    sum_up = jnp.zeros((1, RANK), F32)
    for i in range(2):
        w = halves(wfull[back(x, 2 * i + c, NX), :, :, 0:24, :].reshape(384, RANK))
        right = dot_halves(w, x_up, 1, 1)
        sum_up = sum_up + jnp.sum(right * right, axis=0, keepdims=True)
    ssum[...] = jnp.zeros((8, RANK), F32)
    ssum[0:1, :] = sum_up
    ssum[1:2, :] = sum_down
    s_wait = group(120)
    phase[0] = 4
    for d in FAR_FIRST + (0,):
        zz = lax.rem(z + d, NZ)
        transfer(ssum, ssum_in.at[8 * c + d], at(x, y, 1 - c, zz), s_wait)
        if d:
            transfer(ssum, ssum_in.at[8 * c + d], at(x, y, c, zz), s_wait)
    ssum_in[8 * c] = ssum[...]
    o_up = dot_halves(halves(p_up), x_up, 1, 1)
    o_down = dot_halves(halves(p_down), x_down, 1, 1)
    z_up = halves(dot_halves(halves(o_up), x_up))
    z_down = halves(dot_halves(halves(o_down), x_down))
    wd_all = (wd_half[0].reshape(384, RANK), wd_half[1].reshape(384, RANK))
    writes = []

    def write(src, dst):
        copy = pltpu.make_async_copy(src, dst, local.at[4 + len(writes)])
        copy.start()
        writes.append(copy)

    o_new_down[...] = blend_down[...] - (1.0 - retain) * dot_halves(z_down, wd_all, 1, 1)
    write(o_new_down, new_down)
    w_halves = []
    for g in range(NX):
        cols = slice(384 * g, 384 * g + 384)
        w_halves.append(halves(wfull[g, :, :, 0:24, :].reshape(384, RANK)))
        o_new_up[:, cols] = blend_up[:, cols] - (1.0 - retain) * dot_halves(
            z_up, w_halves[g], 1, 1
        )
    write(o_new_up, new_up)
    nb_one = dot_halves(halves(wfull[x, y, c, 0:24, :]), x_up, 1, 1)
    nb = dot_halves(halves(wfull[x, y, c, 24:32, :]), x_down, 1, 1)
    for n in range(4):
        drain(n)
    s_wait()
    sums = ssum_in[0]
    for i in range(1, 16):
        sums = sums + ssum_in[i]
    scale = lax.rsqrt(sums + epsilon)
    s_up, s_down = scale[0:1], scale[1:2]
    z_up = halves(dot_halves(halves(math.sqrt(3072 / 12288) * o_up * s_up), x_up))
    for g in range(NX):
        o_upd_up[:, 384 * g : 384 * g + 384] = dot_halves(z_up, w_halves[g], 1, 1)
    write(o_upd_up, upd_up)
    z_down = halves(dot_halves(halves(math.sqrt(12288 / 3072) * o_down * s_down), x_down))
    o_upd_down[...] = dot_halves(z_down, wd_all, 1, 1)
    write(o_upd_down, upd_down)
    nb_up[0] = nb_one * s_up
    nb = nb * s_down
    for i in range(6):
        nb_down[i] = nb[i : i + 1]
    drain(4)
    for copy in writes:
        copy.wait()


PIECES = (NX, NY, 2, 32, RANK)
SCRATCH = (
    [PIECES, PIECES, PIECES, (NX, NY, 32, RANK), (NX, NY, 32, RANK)]
    + [(NX - 1, NY, 24, RANK), (NY, 24, RANK), (NY - 1, 24, RANK)]
    + [(NY - 1, NX, 8, RANK), (NX, 8, RANK), (NX - 1, 8, RANK)]
    + [(48, 1536), (192, 384), (48, 1536), (192, 384)]
    + [(48, 1536), (48, 1536), (192, 384), (192, 384)]
    + [(NZ, 8, RANK), (NZ - 1, 8, RANK), (NZ, 8, RANK)]
    + [(NZ, 24, RANK), (NZ - 1, 24, RANK), (NZ, 24, RANK)]
    + [(RANK, 48), (RANK, 192), (2, 32, RANK), (32, RANK), (NX, 8, RANK), (NX - 1, 8, RANK), (NY, 8, RANK)]
    + [(NZ, NX, 8, RANK)]
    + [(2, RANK, RANK), (8, RANK), (16, 8, RANK), (4096, 128)]
)
HALF_SCRATCH = (
    [(48, 1536), (192, 384)]
    + [(NX, 48, 384)] * 2
    + [(192, 512)] * 2
    + [(NX, 384, 48)] * 2
    + [(512, 192)] * 2
    + [(2, 2, 192, RANK)]
)
PHASES, GROUPS = 5, 80


def finish(*refs):
    sources, results, held, sems = refs[0:6], refs[6:12], refs[12:18], refs[18]
    reads = [pltpu.make_async_copy(a, b, sems.at[0, i]) for i, (a, b) in enumerate(zip(sources, held))]
    writes = [pltpu.make_async_copy(a, b, sems.at[1, i]) for i, (a, b) in enumerate(zip(held, results))]
    for copy in reads:
        copy.start()
    for read, write in zip(reads, writes):
        read.wait()
        write.start()
    for copy in writes:
        copy.wait()


def body(mom_up, grad_up, basis_up, mom_down, grad_down, basis_down):
    vmem = pl.BlockSpec(memory_space=pltpu.VMEM)
    anywhere = pl.BlockSpec(memory_space=pl.ANY)
    shapes = [(48, 1536), (48, 1536), (1, 24, RANK), (192, 384), (192, 384), (6, 1, RANK)]
    out_shape = [jax.ShapeDtypeStruct(s, F32) for s in shapes]
    results = pl.pallas_call(
        kernel,
        out_shape=out_shape,
        in_specs=[anywhere, anywhere, vmem] * 2,
        out_specs=[anywhere, anywhere, vmem] * 2,
        scratch_shapes=[pltpu.VMEM(s, F32) for s in SCRATCH]
        + [pltpu.VMEM(s, jnp.bfloat16) for s in HALF_SCRATCH]
        + [pltpu.SemaphoreType.DMA((n,)) for n in (PHASES, GROUPS)]
        + [pltpu.SemaphoreType.DMA((8,))],
        compiler_params=pltpu.CompilerParams(
            collective_id=0, has_side_effects=True, vmem_limit_bytes=60 << 20
        ),
    )(mom_up, grad_up, basis_up, mom_down, grad_down, jnp.swapaxes(basis_down, 0, 1))
    results = pl.pallas_call(
        finish,
        out_shape=out_shape,
        in_specs=[anywhere] * 6,
        out_specs=[anywhere] * 6,
        scratch_shapes=[pltpu.VMEM(s, F32) for s in shapes] + [pltpu.SemaphoreType.DMA((2, 6))],
    )(*results)
    return (*results[:5], jnp.swapaxes(results[5], 0, 1))


def solution(mesh):
    specs = (P("fsdp", "tp"), P("fsdp", "tp"), P("tp", "fsdp", None)) * 2
    return jax.shard_map(
        body,
        mesh=mesh,
        in_specs=specs,
        out_specs=specs,
        check_vma=False,
    )
```

```python
import math

import jax
import jax.numpy as jnp
from jax import lax
from jax.experimental import pallas as pl
from jax.experimental.pallas import tpu as pltpu
from jax.sharding import PartitionSpec as P

retain = 0.9
epsilon = 1e-06
HIGH = lax.Precision.HIGHEST
MESH = pl.DeviceIdType.MESH
NX, NY, NZ, RANK = 4, 8, 8, 256
F32 = jnp.float32


def dot(a, b, ca=1, cb=0):
    return lax.dot_general(
        a, b, (((ca,), (cb,)), ((), ())), precision=HIGH, preferred_element_type=F32
    )


def halves(v):
    high = v.astype(jnp.bfloat16)
    return high, (v - high.astype(F32)).astype(jnp.bfloat16)


def dot_halves(a, b, ca=1, cb=0):
    dims = (((ca,), (cb,)), ((), ()))

    def one(u, v):
        return lax.dot_general(u, v, dims, preferred_element_type=F32)

    return one(a[0], b[0]) + (one(a[0], b[1]) + one(a[1], b[0]))


def invert_half(a, hook=None):
    lanes = lax.broadcasted_iota(jnp.int32, (8, 128), 1)
    subs = lax.broadcasted_iota(jnp.int32, (8, 128), 0)
    groups = [a[8 * g : 8 * g + 8] for g in range(16)]
    done = []
    for k in range(16):
        base = 8 * k
        inside = (lanes >= base) & (lanes < base + 8)
        panel = groups[0]
        cols = [jnp.broadcast_to(panel[:, base + j : base + j + 1], (8, 128)) for j in range(8)]
        held = jnp.where(inside, (lanes == subs + base).astype(F32), panel)
        pivots = cols[0]
        inverse, heads = [], []
        for j in range(8):
            r = 1.0 / cols[j][j : j + 1]
            inverse.append(r)
            mult = jnp.where(subs > j, cols[j] * r, 0.0)
            heads.append([c[j : j + 1] for c in cols])
            for jj in range(j + 1, 8):
                cols[jj] = cols[jj] - mult * heads[j][jj]
            held = held - mult * held[j : j + 1]
            if j:
                pivots = jnp.where(subs == j, cols[j], pivots)
        done.append(jnp.where(lanes <= subs + base, held * lax.rsqrt(pivots), 0.0))
        rest = []
        for g in groups[1:]:
            c = [jnp.broadcast_to(g[:, base + j : base + j + 1], (8, 128)) for j in range(8)]
            out = jnp.where(inside, 0.0, g)
            for j in range(8):
                m = c[j] * inverse[j]
                for jj in range(j + 1, 8):
                    c[jj] = c[jj] - m * heads[j][jj]
                out = out - m * held[j : j + 1]
            rest.append(out)
        groups = rest
        if hook is not None:
            hook(k)
    return jnp.concatenate(done, axis=0)


def place():
    f = lax.axis_index("fsdp")
    return f // 16, lax.rem(f // 2, 8), lax.rem(f, 2), lax.axis_index("tp")


NEAR_FIRST = (1, 7, 2, 6, 3, 5, 4)
FAR_FIRST = (4, 3, 5, 2, 6, 1, 7)


def kernel(
    mom_up, grad_up, basis_up, mom_down, grad_down, basis_down,
    upd_up, new_up, nb_up, upd_down, new_down, nb_down,
    q, wfull, wpart, wcore, wsum, wu_x, wu_s, wu_y, wd_y, wd_s, wd_x,
    m_up, m_down, blend_up, blend_down, o_upd_up, o_new_up, o_upd_down, o_new_down,
    part_up, part_up_in, pfull_up, part_down, part_down_in, pfull_down,
    turned_up, turned_down, gram, gram_in, gsum, g_x, g_y, g_all, xinv, ssum, ssum_in, whole,
    g_up, g_down, bu_hi, bu_lo, pd_hi, pd_lo, tu_hi, tu_lo, td_hi, td_lo, wd_half,
    send, recv, local,
):
    x, y, c, z = place()
    count = [0]

    def at(xx, yy, cc, zz):
        return (xx * 16 + yy * 2 + cc, zz)

    def along_y(d):
        return at(x, lax.rem(y + d, NY), c, z)

    def along_x(d):
        return at(lax.rem(x + d, NX), y, c, z)

    def along_z(d):
        return at(x, y, c, lax.rem(z + d, NZ))

    sibling = at(x, y, 1 - c, z)

    barrier = pltpu.get_barrier_semaphore()
    peers = (
        [along_y(d) for d in range(1, NY)]
        + [along_x(d) for d in range(1, NX)]
        + [along_z(d) for d in range(1, NZ)]
        + [at(x, y, 1 - c, lax.rem(z + d, NZ)) for d in range(1, NZ)]
        + [sibling]
    )
    for peer in peers:
        pl.semaphore_signal(barrier, inc=1, device_id=peer, device_id_type=MESH)
    loads = [
        pltpu.make_async_copy(src, dst, local.at[i])
        for i, (src, dst) in enumerate(
            ((mom_down, m_down), (grad_down, g_down), (mom_up, m_up), (grad_up, g_up))
        )
    ]
    for load in loads:
        load.start()

    sent = [0] * PHASES
    phase = [0]

    def group(rows):
        n = count[0]
        count[0] += 1

        def arrive(part=1):
            pltpu.make_async_remote_copy(
                whole.at[0 : 2 * rows // part], whole.at[0 : 2 * rows // part], send.at[0], recv.at[n],
                device_id=sibling, device_id_type=MESH,
            ).wait_recv()

        arrive.number = n
        return arrive

    def transfer(src, dst, device, to):
        pltpu.make_async_remote_copy(
            src, dst, send.at[phase[0]], recv.at[to.number], device_id=device, device_id_type=MESH
        ).start()
        sent[phase[0]] += math.prod(src.shape) // 128

    def drain(n):
        pltpu.make_async_remote_copy(
            whole.at[0 : sent[n]], whole.at[0 : sent[n]], send.at[n], recv.at[0],
            device_id=sibling, device_id_type=MESH,
        ).wait_send()

    def back(v, d, n):
        return lax.rem(v + n - d, n)

    down_x = group(24)
    down_y = group(224)
    up_y = [{d: group(24) for d in NEAR_FIRST} for _ in range(2)]
    up_x = [{d: group(192) for d in range(1, NX)} for _ in range(2)]
    cores = [[group(192) for _ in range(NX)] for _ in range(2)]
    core_rest = group(256)

    class Up:
        def __init__(self, buf, lanes, half, part):
            self.buf, self.lanes, self.part = buf, lanes, part
            self.y, self.x, self.cores, self.seen = up_y[half], up_x[half], cores[half], []
            for d in NEAR_FIRST:
                piece = buf.at[x, y, c, 0:24, lanes]
                transfer(piece, piece, along_y(d), self.y[d])
            self.forward(y)

        def forward(self, yy):
            for d in (2, 1, 3):
                piece = self.buf.at[x, yy, c, 0:24, self.lanes]
                transfer(piece, piece, along_x(d), self.x[d])

        def relay(self, *steps):
            for d in steps:
                self.y[d](self.part)
                self.forward(back(y, d, NY))

        def column(self, *steps):
            for d in steps:
                if d in self.seen:
                    continue
                if d:
                    self.x[d](self.part)
                self.seen.append(d)
                block = self.buf.at[back(x, d, NX), :, c, 0:24, self.lanes]
                transfer(block, block, sibling, self.cores[d])

        def arrive(self, d):
            self.cores[d](self.part)

    class Down:
        def __init__(self, buf):
            self.buf = buf
            for d in (2, 1, 3):
                piece = buf.at[x, y, c, 24:32]
                transfer(piece, piece, along_x(d), down_x)

        def turn(self):
            down_x()
            for d in FAR_FIRST:
                piece = self.buf.at[:, y, c, 24:32]
                transfer(piece, piece, along_y(d), down_y)

        def across(self):
            down_y()
            block = self.buf.at[:, :, c, 24:32]
            transfer(block, block, sibling, core_rest)

    def collect(parts, use):
        before = 0
        for d in (1, 3, 2):
            for part in parts:
                part.column(d)
            for part in parts:
                part.arrive(before)
            use(back(x, before, NX))
            before = d
        for part in parts:
            part.arrive(before)
        use(back(x, before, NX))

    q[x, y, c, 0:24, :] = basis_up[0]
    q[x, y, c, 24:32, :] = jnp.zeros((8, RANK), F32)
    for i in range(6):
        q[x, y, c, 24 + i : 25 + i, :] = basis_down[i]
    pl.semaphore_wait(barrier, len(peers))
    first_down = Down(q)
    first_up = Up(q, slice(0, RANK), 0, 1)

    column = lax.broadcasted_iota(jnp.int32, (384, 512), 0)
    slot = lax.broadcasted_iota(jnp.int32, (384, 512), 1)
    pick = ((column == (slot // 8) * 6 + lax.rem(slot, 8)) & (lax.rem(slot, 8) < 6)).astype(F32)
    for load in loads:
        load.wait()
    blend_down[...] = m_down[...] + g_down[...].astype(F32)
    blend_up[...] = m_up[...] + g_up[...].astype(F32)
    for g in range(NX):
        bu_hi[g], bu_lo[g] = halves(blend_up[:, 384 * g : 384 * g + 384])
    padded = dot(blend_down[...], pick)
    pd_hi[...], pd_lo[...] = halves(padded)
    first_down.turn()
    first_up.relay(*NEAR_FIRST)
    first_up.column(0)
    first_down.across()
    sums_up = []

    def add_up(g):
        piece = halves(q[g, :, :, 0:24, :].reshape(384, RANK))
        sums_up.append(dot_halves((bu_hi[g], bu_lo[g]), piece))

    first_up.arrive(0)
    add_up(x)
    core_rest()
    phase[0] = 1

    p_part = dot_halves(
        (pd_hi[...], pd_lo[...]), halves(q[:, :, :, 24:32, :].reshape(512, RANK))
    )
    part_down[...] = p_part.reshape(NZ, 24, RANK)

    def reduce_z(part, part_in, to):
        for d in FAR_FIRST:
            transfer(part.at[lax.rem(z + d, NZ)], part_in.at[d - 1], along_z(d), to)

    def gather_z(part, part_in, full, to):
        total = part[z]
        for d in range(1, NZ):
            total = total + part_in[d - 1]
        full[z] = total
        for d in FAR_FIRST:
            transfer(full.at[z], full.at[z], along_z(d), to)

    down_rs, down_ag, up_rs, up_ag = group(168), group(168), group(56), group(56)
    reduce_z(part_down, part_down_in, down_rs)

    phase[0] = 0
    first_up.column(1, 3)
    for d in (1, 3):
        first_up.arrive(d)
        add_up(back(x, d, NX))
    first_up.column(2)
    first_up.arrive(2)
    add_up(back(x, 2, NX))
    phase[0] = 1
    part_up[0:6] = (sums_up[0] + sums_up[1] + sums_up[2] + sums_up[3]).reshape(6, 8, RANK)
    part_up[6:8] = jnp.zeros((2, 8, RANK), F32)
    reduce_z(part_up, part_up_in, up_rs)
    for g in range(NX):
        tu_hi[g], tu_lo[g] = halves(blend_up[:, 384 * g : 384 * g + 384].T)
    td_hi[...], td_lo[...] = halves(padded.T)
    down_rs()
    gather_z(part_down, part_down_in, pfull_down, down_ag)
    up_rs()
    gather_z(part_up, part_up_in, pfull_up, up_ag)

    down_ag()
    p_down = pfull_down[...].reshape(192, RANK)
    rows = pl.ds(pl.multiple_of(32 * z, 8), 32)
    turned_down[...] = p_down.T
    gram[1] = dot(turned_down[rows, :], p_down)
    up_ag()
    p_up = pfull_up[0:6].reshape(48, RANK)
    turned_up[...] = p_up.T
    gram[0] = dot(turned_up[rows, :], p_up)
    gram_core, gram_x, gram_y, gram_z, gram_all = [group(n) for n in (32, 24, 56, 56, 144)]
    transfer(gram.at[1 - c], gram_in, sibling, gram_core)
    p_halves = halves(p_up)
    core_up = [group(192) for _ in range(NX)]
    core_down = group(256)
    w_x = [[group(36) for _ in range(NY)] for _ in range(2)]
    w_y = [group(84), group(84)]
    wd_y_all, wd_x_all = group(224), group(24)
    sides = [slice(0, 128), slice(128, 256)]

    def multiply(e):
        g = lax.rem(x + e, NX)
        wpart[g, :, :, 0:24, :] = dot_halves((tu_hi[g], tu_lo[g]), p_halves).reshape(
            NY, 2, 24, RANK
        )
        phase[0] = 2
        transfer(wpart.at[g, :, 1 - c, 0:24], wcore.at[g, :, 0:24], sibling, core_up[e])
        phase[0] = 1

    def join(e):
        g = lax.rem(x + e, NX)
        core_up[e]()
        wsum[g, :, 0:24] = wpart[g, :, c, 0:24] + wcore[g, :, 0:24]

    def scatter_x(e, d, h):
        phase[0] = 2
        transfer(
            wsum.at[lax.rem(x + e, NX), lax.rem(y + d, NY), 0:24, sides[h]],
            wu_x.at[e - 1, d, :, sides[h]], along_x(e), w_x[h][d],
        )
        phase[0] = 1

    def scatter_y(h, *steps):
        lanes = sides[h]
        for d in steps:
            w_x[h][d]()
            wu_s[d, :, lanes] = (
                wsum[x, lax.rem(y + d, NY), 0:24, lanes]
                + wu_x[0, d, :, lanes] + wu_x[1, d, :, lanes] + wu_x[2, d, :, lanes]
            )
            if d:
                phase[0] = 2
                transfer(wu_s.at[d, :, lanes], wu_y.at[d - 1, :, lanes], along_y(d), w_y[h])
                phase[0] = 1

    def own_piece(h):
        lanes = sides[h]
        w_y[h]()
        owned = wu_s[0, :, lanes]
        for d in range(1, NY):
            owned = owned + wu_y[d - 1, :, lanes]
        wfull[x, y, c, 0:24, lanes] = owned
        phase[0] = 3
        gathers.append(Up(wfull, lanes, h, 2))
        phase[0] = 1

    gathers = []
    multiply(2)
    gram_core()
    gsum[...] = (gram[c] + gram_in[...]).reshape(NX, 8, RANK)
    for d in (2, 1, 3):
        transfer(gsum.at[lax.rem(x + d, NX)], g_x.at[d - 1], along_x(d), gram_x)
    multiply(1)
    multiply(3)
    join(2)
    for d in FAR_FIRST + (0,):
        scatter_x(2, d, 0)
    multiply(0)
    gram_x()
    g_y[y] = gsum[x] + g_x[0] + g_x[1] + g_x[2]
    for d in FAR_FIRST:
        transfer(g_y.at[y], g_y.at[y], along_y(d), gram_y)
    wpart[:, :, :, 24:32, :] = dot_halves((td_hi[...], td_lo[...]), halves(p_down)).reshape(
        NX, NY, 2, 8, RANK
    )
    phase[0] = 2
    transfer(wpart.at[:, :, 1 - c, 24:32], wcore.at[:, :, 24:32], sibling, core_down)
    join(1)
    join(3)
    for d in FAR_FIRST + (0,):
        scatter_x(1, d, 0)
        scatter_x(3, d, 0)
    for d in FAR_FIRST + (0,):
        scatter_x(2, d, 1)
        scatter_x(1, d, 1)
        scatter_x(3, d, 1)
    core_down()
    wsum[:, :, 24:32] = wpart[:, :, c, 24:32] + wcore[:, :, 24:32]
    phase[0] = 2
    for d in FAR_FIRST:
        transfer(wsum.at[:, lax.rem(y + d, NY), 24:32], wd_y.at[d - 1], along_y(d), wd_y_all)
    phase[0] = 1
    join(0)
    gram_y()
    row = g_y[0]
    for i in range(1, NY):
        row = row + g_y[i]
    g_all[z, x] = row
    for d in FAR_FIRST:
        transfer(g_all.at[z, x], g_all.at[z, x], along_z(d), gram_z)
    scatter_y(0, *FAR_FIRST, 0)
    scatter_y(1, *FAR_FIRST[:4])
    gram_z()
    for d in (2, 1, 3):
        for piece in (g_all.at[0:4, x], g_all.at[4:8, x, :, 128:256]):
            transfer(piece, piece, along_x(d), gram_all)
    wd_y_all()
    owned = wsum[:, y, 24:32]
    for d in range(1, NY):
        owned = owned + wd_y[d - 1]
    wd_s[...] = owned
    phase[0] = 2
    for d in (2, 1, 3):
        transfer(wd_s.at[lax.rem(x + d, NX)], wd_x.at[d - 1], along_x(d), wd_x_all)
    phase[0] = 1
    scatter_y(1, *FAR_FIRST[4:], 0)
    own_piece(0)
    wd_x_all()
    wfull[x, y, c, 24:32, :] = wd_s[x] + wd_x[0] + wd_x[1] + wd_x[2]
    phase[0] = 3
    rest = Down(wfull)
    gram_all()

    g11, g12, g22 = (
        g_all[0:4, :, :, 0:128].reshape(128, 128),
        g_all[0:4, :, :, 128:256].reshape(128, 128),
        g_all[4:8, :, :, 128:256].reshape(128, 128),
    )

    def hook(k):
        if k == 2:
            own_piece(1)
            phase[0] = 3
        if k == 3:
            gathers[0].relay(1, 7)
        if k == 5:
            gathers[0].relay(2, 6)
        if k == 7:
            rest.turn()
        if k == 9:
            gathers[1].relay(1, 7)
        if k == 10:
            gathers[0].relay(3, 5, 4)
            gathers[0].column(0)
        if k == 13:
            gathers[1].relay(2, 6)
        if k == 15:
            gathers[1].relay(3, 5)

    x11 = invert_half(g11, hook)
    xinv[c, 0:128, 0:128] = x11
    xinv[c, 0:128, 128:256] = jnp.zeros((128, 128), F32)
    u = dot(x11, g12)
    low = g22 - dot(u, u, 0, 0)
    corner = dot(u, x11, 0, 0)

    late = []

    def hook(k):
        if k == 0:
            gathers[1].relay(4)
            gathers[1].column(0)
        if k == 4:
            gathers[0].column(1, 3)
        if k == 7:
            gathers[0].column(2)
        if k == 11:
            gathers[1].column(1, 3)
        if k == 13:
            rest.across()

    x22 = invert_half(low, hook)
    xinv[c, 128:256, 128:256] = x22
    xinv[c, 128:256, 0:128] = -dot(x22, corner)
    x_wait = group(256)
    phase[0] = 1
    transfer(xinv.at[c], xinv.at[c], sibling, x_wait)
    phase[0] = 3
    core_rest()
    select = pick.astype(jnp.bfloat16)
    for i, half in enumerate(halves(wfull[:, :, :, 24:32, :].reshape(512, RANK))):
        rows = lax.dot_general(
            select, half, (((1,), (0,)), ((), ())), preferred_element_type=F32
        )
        wd_half[i] = rows.astype(jnp.bfloat16).reshape(2, 192, RANK)
    x_wait()
    x_up, x_down = halves(xinv[0]), halves(xinv[1])
    right = dot_halves((wd_half[0, c], wd_half[1, c]), x_down, 1, 1)
    sum_down = jnp.sum(right * right, axis=0, keepdims=True)
    collect(gathers, lambda g: None)
    sum_up = jnp.zeros((1, RANK), F32)
    for i in range(2):
        w = halves(wfull[back(x, 2 * i + c, NX), :, :, 0:24, :].reshape(384, RANK))
        right = dot_halves(w, x_up, 1, 1)
        sum_up = sum_up + jnp.sum(right * right, axis=0, keepdims=True)
    ssum[...] = jnp.zeros((8, RANK), F32)
    ssum[0:1, :] = sum_up
    ssum[1:2, :] = sum_down
    s_wait = group(120)
    phase[0] = 4
    for d in FAR_FIRST + (0,):
        zz = lax.rem(z + d, NZ)
        transfer(ssum, ssum_in.at[8 * c + d], at(x, y, 1 - c, zz), s_wait)
        if d:
            transfer(ssum, ssum_in.at[8 * c + d], at(x, y, c, zz), s_wait)
    ssum_in[8 * c] = ssum[...]
    o_up = dot_halves(halves(p_up), x_up, 1, 1)
    o_down = dot_halves(halves(p_down), x_down, 1, 1)
    z_up = halves(dot_halves(halves(o_up), x_up))
    z_down = halves(dot_halves(halves(o_down), x_down))
    wd_all = (wd_half[0].reshape(384, RANK), wd_half[1].reshape(384, RANK))
    writes = []

    def write(src, dst):
        copy = pltpu.make_async_copy(src, dst, local.at[4 + len(writes)])
        copy.start()
        writes.append(copy)

    o_new_down[...] = blend_down[...] - (1.0 - retain) * dot_halves(z_down, wd_all, 1, 1)
    write(o_new_down, new_down)
    w_halves = []
    for g in range(NX):
        cols = slice(384 * g, 384 * g + 384)
        w_halves.append(halves(wfull[g, :, :, 0:24, :].reshape(384, RANK)))
        o_new_up[:, cols] = blend_up[:, cols] - (1.0 - retain) * dot_halves(
            z_up, w_halves[g], 1, 1
        )
    write(o_new_up, new_up)
    nb_one = dot_halves(halves(wfull[x, y, c, 0:24, :]), x_up, 1, 1)
    nb = dot_halves(halves(wfull[x, y, c, 24:32, :]), x_down, 1, 1)
    for n in range(4):
        drain(n)
    s_wait()
    sums = ssum_in[0]
    for i in range(1, 16):
        sums = sums + ssum_in[i]
    scale = lax.rsqrt(sums + epsilon)
    s_up, s_down = scale[0:1], scale[1:2]
    z_up = halves(dot_halves(halves(math.sqrt(3072 / 12288) * o_up * s_up), x_up))
    for g in range(NX):
        o_upd_up[:, 384 * g : 384 * g + 384] = dot_halves(z_up, w_halves[g], 1, 1)
    write(o_upd_up, upd_up)
    z_down = halves(dot_halves(halves(math.sqrt(12288 / 3072) * o_down * s_down), x_down))
    o_upd_down[...] = dot_halves(z_down, wd_all, 1, 1)
    write(o_upd_down, upd_down)
    nb_up[0] = nb_one * s_up
    nb = nb * s_down
    for i in range(6):
        nb_down[i] = nb[i : i + 1]
    drain(4)
    for copy in writes:
        copy.wait()


PIECES = (NX, NY, 2, 32, RANK)
SCRATCH = (
    [PIECES, PIECES, PIECES, (NX, NY, 32, RANK), (NX, NY, 32, RANK)]
    + [(NX - 1, NY, 24, RANK), (NY, 24, RANK), (NY - 1, 24, RANK)]
    + [(NY - 1, NX, 8, RANK), (NX, 8, RANK), (NX - 1, 8, RANK)]
    + [(48, 1536), (192, 384), (48, 1536), (192, 384)]
    + [(48, 1536), (48, 1536), (192, 384), (192, 384)]
    + [(NZ, 8, RANK), (NZ - 1, 8, RANK), (NZ, 8, RANK)]
    + [(NZ, 24, RANK), (NZ - 1, 24, RANK), (NZ, 24, RANK)]
    + [(RANK, 48), (RANK, 192), (2, 32, RANK), (32, RANK), (NX, 8, RANK), (NX - 1, 8, RANK), (NY, 8, RANK)]
    + [(NZ, NX, 8, RANK)]
    + [(2, RANK, RANK), (8, RANK), (16, 8, RANK), (4096, 128)]
)
HALF_SCRATCH = (
    [(48, 1536), (192, 384)]
    + [(NX, 48, 384)] * 2
    + [(192, 512)] * 2
    + [(NX, 384, 48)] * 2
    + [(512, 192)] * 2
    + [(2, 2, 192, RANK)]
)
PHASES, GROUPS = 5, 80


def finish(*refs):
    sources, results, held, sems = refs[0:6], refs[6:12], refs[12:18], refs[18]
    reads = [pltpu.make_async_copy(a, b, sems.at[0, i]) for i, (a, b) in enumerate(zip(sources, held))]
    writes = [pltpu.make_async_copy(a, b, sems.at[1, i]) for i, (a, b) in enumerate(zip(held, results))]
    for copy in reads:
        copy.start()
    for read, write in zip(reads, writes):
        read.wait()
        write.start()
    for copy in writes:
        copy.wait()


def body(mom_up, grad_up, basis_up, mom_down, grad_down, basis_down):
    vmem = pl.BlockSpec(memory_space=pltpu.VMEM)
    anywhere = pl.BlockSpec(memory_space=pl.ANY)
    shapes = [(48, 1536), (48, 1536), (1, 24, RANK), (192, 384), (192, 384), (6, 1, RANK)]
    out_shape = [jax.ShapeDtypeStruct(s, F32) for s in shapes]
    results = pl.pallas_call(
        kernel,
        out_shape=out_shape,
        in_specs=[anywhere, anywhere, vmem] * 2,
        out_specs=[anywhere, anywhere, vmem] * 2,
        scratch_shapes=[pltpu.VMEM(s, F32) for s in SCRATCH]
        + [pltpu.VMEM(s, jnp.bfloat16) for s in HALF_SCRATCH]
        + [pltpu.SemaphoreType.DMA((n,)) for n in (PHASES, GROUPS)]
        + [pltpu.SemaphoreType.DMA((8,))],
        compiler_params=pltpu.CompilerParams(
            collective_id=0, has_side_effects=True, vmem_limit_bytes=60 << 20
        ),
    )(mom_up, grad_up, basis_up, mom_down, grad_down, jnp.swapaxes(basis_down, 0, 1))
    results = pl.pallas_call(
        finish,
        out_shape=out_shape,
        in_specs=[anywhere] * 6,
        out_specs=[anywhere] * 6,
        scratch_shapes=[pltpu.VMEM(s, F32) for s in shapes] + [pltpu.SemaphoreType.DMA((2, 6))],
    )(*results)
    return (*results[:5], jnp.swapaxes(results[5], 0, 1))


def solution(mesh):
    specs = (P("fsdp", "tp"), P("fsdp", "tp"), P("tp", "fsdp", None)) * 2
    return jax.shard_map(
        body,
        mesh=mesh,
        in_specs=specs,
        out_specs=specs,
        check_vma=False,
    )
```
